128 devices in a mesh: section: 4 (over z), row: 8 (over x, core), col: 4 (over y).
Axes of the slice: x: 4, y: 4, z: 4, core: 2. Of those that a mesh axis runs over, the one named last changes fastest.
Arguments:
- hidden: bfloat16 [4, 64, 5120], P('section', None, ('row', 'col')), may hold values from -64 to 64
- lengths: int32 [4, 64], P(None, 'row'), may hold values from 24 to 96, as said below
- attn_gain: bfloat16 [4, 5120], P('section', ('row', 'col')), may hold values from 0.099609375 to 1.8984375
- ffn_gain: bfloat16 [4, 5120], P('section', ('row', 'col')), may hold values from 0.099609375 to 1.8984375
- q_weight: bfloat16 [4, 5120, 5120], P('section', 'row', 'col'), may hold values from -0.078125 to 0.078125
- key_weight: bfloat16 [4, 5120, 1024], P('section', 'row', 'col'), may hold values from -0.078125 to 0.078125
- value_weight: bfloat16 [4, 5120, 1024], P('section', 'row', 'col'), may hold values from -0.078125 to 0.078125
- out_weight: bfloat16 [4, 5120, 5120], P('section', 'col', 'row'), may hold values from -0.125 to 0.125
- gate_weight: bfloat16 [4, 5120, 16384], P('section', None, ('row', 'col')), may hold values from -0.078125 to 0.078125
- up_weight: bfloat16 [4, 5120, 16384], P('section', None, ('row', 'col')), may hold values from -0.078125 to 0.078125
- down_weight: bfloat16 [4, 16384, 5120], P('section', ('row', 'col')), may hold values from -0.09375 to 0.09375
- key_cache: bfloat16 [4, 4, 64, 8, 96, 128], P('section', None, 'row', 'col'), may hold values from -256 to 256
- value_cache: bfloat16 [4, 4, 64, 8, 96, 128], P('section', None, 'row', 'col'), may hold values from -6 to 6
Outputs:
- states: bfloat16 [4, 64, 5120], P('section', None, ('row', 'col'))
The draws below stay inside these ranges and needn't reach their ends.
Inputs may be any that keep to these rules, and one draw needn't show every extreme that they name: `lengths`: in every micro-batch one stream has exactly 96 cached positions and another exactly 24.
All inputs are finite; a program needn't handle non-finite values.
Results may differ from the reference program's by a relative error of at most 0.035.
Values may be sent and summed in bfloat16 or wider, within the bound.
A program may use at most 128 MiB of HBM per device.

```python
import math
import jax
import jax.numpy as jnp
from jax import lax

D = 5120
HEADS = 40
KVH = 8
HD = 128
FFW = 16384
B = 64
CTX = 96
MB = 4
QD = 5120
KD = 1024
N_SECTION = 4


def draw_hidden(key, part):
    key = jax.random.fold_in(key, 5)
    keys = jax.random.split(key, 3)
    row_scale = 10.0 ** (0.5 * (jax.random.uniform(keys[0], (MB, B, 1)) - 0.5))
    rising = 3.0 ** (jnp.arange(D, dtype=jnp.float32) / D - 0.5)
    col_scale = 10.0 ** (0.5 * (jax.random.uniform(keys[1], (1, 1, D)) - 0.5)) * rising[None, None, :]
    base = jnp.clip(jax.random.normal(keys[2], (MB, B, D)), -5.0, 5.0)
    return (base * row_scale * col_scale).astype(jnp.bfloat16)


def draw_lengths(key, part):
    key = jax.random.fold_in(key, 11)
    keys = jax.random.split(key, 3)
    base = jax.random.randint(keys[0], (MB, B), CTX // 4, CTX + 1)
    longest = jax.random.randint(keys[1], (MB, 1), 0, B)
    shortest = (longest + 1 + jax.random.randint(keys[2], (MB, 1), 0, B - 1)) % B
    columns = jnp.arange(B, dtype=jnp.int32)[None, :]
    base = jnp.where(columns == longest, CTX, base)
    base = jnp.where(columns == shortest, CTX // 4, base)
    return base.astype(jnp.int32)


def draw_key_cache(key, part):
    key = jax.random.fold_in(key, 7)
    keys = jax.random.split(key, 1)
    shape = (N_SECTION, MB, B, KVH, CTX, HD)
    base = jnp.clip(jax.random.normal(keys[0], shape), -4.0, 4.0)
    return base.astype(jnp.bfloat16)


def strengthened(result, own_key, source, target, shards_of, factor):
    def block_of(dim):
        return (jnp.arange(result.shape[dim]) // (result.shape[dim] // shards_of)).reshape((-1,) + (1,) * (result.ndim - 1 - dim))

    first = jax.random.permutation(own_key, shards_of)[block_of(target)]
    far = (block_of(target) + shards_of // 2) % shards_of
    return jnp.where((block_of(source) == first) | (block_of(source) == far), factor * result, result)


def shard_levels(stream_key, dims, pieces, smallest, high):
    def one(axis_at, parts):
        steps = jax.random.uniform(jax.random.fold_in(jax.random.fold_in(stream_key, 6), axis_at), (parts,), jnp.float32, smallest / len(pieces), high / len(pieces))
        return jnp.repeat(jnp.exp(steps), dims[axis_at] // parts).reshape((-1,) + (1,) * (len(dims) - axis_at - 1))

    level = one(*pieces[0])
    for cut in pieces[1:]:
        level = level * one(*cut)
    return level


def gaussian(stream_key, extent, width, bound, pieces=(), held_as=jnp.bfloat16):
    entries = jax.random.normal(stream_key, extent, jnp.float32) * width
    if len(pieces) > 0:
        entries = shard_levels(stream_key, extent, pieces, -0.22, 0.18) * entries
    return jnp.clip(entries, min=-bound, max=bound).astype(held_as)


def gaussian_with(key, dims, scale, limit, pieces, heavy, kind=jnp.bfloat16):
    entries = scale * jax.random.normal(key, dims, jnp.float32)
    if pieces:
        entries = entries * shard_levels(key, dims, pieces, -0.22, 0.18)
    return jnp.clip(strengthened(entries, jax.random.fold_in(key, 3), *heavy), -limit, limit).astype(kind)


def setup_inputs(seed: int = 0) -> dict:
    key_list = jax.random.split(jax.random.key(seed), 14)
    hidden = draw_hidden(jax.random.fold_in(key_list[13], 71), 0)
    lengths = draw_lengths(jax.random.fold_in(key_list[13], 71), 0)
    attn_gain = jnp.clip(1.0 + 0.18 * jax.random.normal(key_list[2], (N_SECTION, D), jnp.float32), 0.099609375, 1.8984375).astype(jnp.bfloat16)
    ffn_gain = jnp.clip(1.0 + 0.18 * jax.random.normal(key_list[3], (N_SECTION, D), jnp.float32), 0.099609375, 1.8984375).astype(jnp.bfloat16)
    q_weight = gaussian(key_list[4], (N_SECTION, D, QD), D ** -0.5, 0.078125, ((0, 4), (1, 8), (2, 4)))
    key_weight = gaussian(key_list[5], (N_SECTION, D, KD), D ** -0.5, 0.078125, ((0, 4), (1, 8), (2, 4)))
    value_weight = gaussian(key_list[6], (N_SECTION, D, KD), D ** -0.5, 0.078125, ((0, 4), (1, 8), (2, 4)))
    out_weight = gaussian_with(key_list[7], (N_SECTION, QD, D), QD ** -0.5, 0.125, ((0, 4), (1, 4), (2, 8)), (1, 2, 8, 2.0))
    gate_weight = gaussian(key_list[8], (N_SECTION, D, FFW), D ** -0.5, 0.078125, ((0, 4), (2, 32)))
    up_weight = gaussian(key_list[9], (N_SECTION, D, FFW), D ** -0.5, 0.078125, ((0, 4), (2, 32)))
    down_weight = gaussian_with(key_list[10], (N_SECTION, FFW, D), FFW ** -0.5, 0.09375, ((0, 4), (1, 32)), (1, 2, 32, 2.75))
    key_cache = draw_key_cache(jax.random.fold_in(key_list[13], 71), 0)
    value_cache = gaussian(key_list[12], (N_SECTION, MB, B, KVH, CTX, HD), 1.0, 6.0, ((0, 4), (2, 8), (3, 4)))
    return dict(hidden=hidden, lengths=lengths, attn_gain=attn_gain, ffn_gain=ffn_gain, q_weight=q_weight, key_weight=key_weight, value_weight=value_weight, out_weight=out_weight, gate_weight=gate_weight, up_weight=up_weight, down_weight=down_weight, key_cache=key_cache, value_cache=value_cache)


norm_eps = 1e-06
masked_score = -1e+30

def normalized(stream_state, gain_row):
    values_f32 = stream_state.astype(jnp.float32)
    mean_square = lax.optimization_barrier(jnp.mean(values_f32 * values_f32, axis=-1, keepdims=True))
    return (values_f32 * lax.rsqrt(mean_square + norm_eps) * gain_row.astype(jnp.float32)).astype(jnp.bfloat16)

def attention(queries, new_keys, new_values, cached_keys, cached_values, live_lengths):
    streams = queries.shape[0]
    per_group = HEADS // KVH
    query_tiles = queries.astype(jnp.float32).reshape(streams, KVH, per_group, HD)
    key_new = new_keys.astype(jnp.float32).reshape(streams, KVH, HD)
    value_new = new_values.astype(jnp.float32).reshape(streams, KVH, HD)
    score_scale = 1.0 / math.sqrt(HD)
    scores = jnp.einsum('bgqd,bgtd->bgqt', query_tiles, cached_keys.astype(jnp.float32)) * score_scale
    self_score = jnp.einsum('bgqd,bgd->bgq', query_tiles, key_new) * score_scale
    positions = jnp.arange(CTX, dtype=jnp.int32)
    valid = positions[None, :] < live_lengths.astype(jnp.int32)[:, None]
    scores = jnp.where(valid[:, None, None, :], scores, masked_score)
    row_max = jnp.maximum(lax.optimization_barrier(jnp.max(scores, axis=-1)), self_score)
    weights = jnp.exp(scores - row_max[..., None])
    self_weight = jnp.exp(self_score - row_max)
    denominator = lax.optimization_barrier(jnp.sum(weights, axis=-1)) + self_weight
    probs = (weights / denominator[..., None]).astype(jnp.bfloat16)
    self_prob = (self_weight / denominator).astype(jnp.bfloat16)
    mixed = jnp.einsum('bgqt,bgtd->bgqd', probs.astype(jnp.float32), cached_values.astype(jnp.float32))
    mixed = mixed + self_prob.astype(jnp.float32)[..., None] * value_new[:, :, None, :]
    return mixed.reshape(streams, HEADS * HD).astype(jnp.bfloat16)

def product(left, right):
    return jnp.dot(left, right, preferred_element_type=jnp.float32)

def reference(hidden, lengths, attn_gain, ffn_gain, q_weight, key_weight, value_weight, out_weight, gate_weight, up_weight, down_weight, key_cache, value_cache):
    results = []
    for micro_batch in range(MB):
        current = hidden[micro_batch]
        for step_index in range(N_SECTION):
            layer_index = (micro_batch + step_index) % N_SECTION
            first_in = normalized(current, attn_gain[layer_index])
            queries = product(first_in, q_weight[layer_index]).astype(jnp.bfloat16)
            new_keys = product(first_in, key_weight[layer_index]).astype(jnp.bfloat16)
            new_values = product(first_in, value_weight[layer_index]).astype(jnp.bfloat16)
            attended = attention(queries, new_keys, new_values, key_cache[layer_index, micro_batch], value_cache[layer_index, micro_batch], lengths[micro_batch])
            after_attn = (current.astype(jnp.float32) + product(attended, out_weight[layer_index])).astype(jnp.bfloat16)
            second_in = normalized(after_attn, ffn_gain[layer_index])
            gate_val = product(second_in, gate_weight[layer_index])
            up_val = product(second_in, up_weight[layer_index])
            activation = (jax.nn.silu(gate_val) * up_val).astype(jnp.bfloat16)
            current = (after_attn.astype(jnp.float32) + product(activation, down_weight[layer_index])).astype(jnp.bfloat16)
        results.append(current)
    return jnp.stack(results)
```

```python
import functools
import math

import jax
import jax.numpy as jnp
from jax import lax
from jax.experimental import pallas as pl
from jax.experimental.pallas import tpu as pltpu
from jax.sharding import PartitionSpec as P

D = 5120
HD = 128
CTX = 96
TURNS = 4
ROWS = 8
COLS = 4
GROUP = ROWS * COLS
WIDE = 640
PIECE = 160
SUB = 16
STREAMS = 64
LOCAL = 8
QKV = 1792
HALF = 896
HIDDEN = 512
norm_eps = 1e-06
masked_score = -1e30
f32 = jnp.float32
bf16 = jnp.bfloat16


def remote(src, dst, send, recv, device):
    return pltpu.make_async_remote_copy(
        src_ref=src,
        dst_ref=dst,
        send_sem=send,
        recv_sem=recv,
        device_id=device,
        device_id_type=pl.DeviceIdType.MESH,
    )


def kernel(
    len_ref,
    hid_ref,
    ag_ref,
    fg_ref,
    wq_hbm,
    wk_hbm,
    wv_hbm,
    wo_hbm,
    wg_hbm,
    wu_hbm,
    wd_hbm,
    kc_hbm,
    vc_hbm,
    out_ref,
    wqkv,
    wo,
    wgu,
    wd,
    kc,
    vc,
    init,
    gain1,
    gain2,
    bias,
    xin,
    s2,
    r2,
    o3,
    s4,
    r4,
    x2_all,
    acc,
    s6,
    r6,
    x_send,
    wsem,
    csem,
    send0,
    recv0,
    sendg,
    recvg,
    send1,
    recv1,
    send2,
    recv2,
    send3,
    recv3,
    send4,
    recv4,
    send5,
    recv5,
    send6,
    recv6,
):
    s = lax.axis_index("section")
    r = lax.axis_index("row")
    c = lax.axis_index("col")
    me = r * COLS + c
    x_chip = r // 2
    s_next = lax.rem(s + 1, TURNS)
    s_prev = lax.rem(s + TURNS - 1, TURNS)

    def row_at(i):
        return lax.rem(r + i, ROWS)

    def col_at(i):
        return lax.rem(c + i, COLS)

    weight_copies = [
        pltpu.make_async_copy(wq_hbm.at[0], wqkv.at[:, pl.ds(0, 1280)], wsem.at[0]),
        pltpu.make_async_copy(wk_hbm.at[0], wqkv.at[:, pl.ds(1280, 256)], wsem.at[1]),
        pltpu.make_async_copy(wv_hbm.at[0], wqkv.at[:, pl.ds(1536, 256)], wsem.at[2]),
        pltpu.make_async_copy(wo_hbm.at[0], wo, wsem.at[3]),
        pltpu.make_async_copy(wg_hbm.at[0], wgu.at[:, pl.ds(0, HIDDEN)], wsem.at[4]),
        pltpu.make_async_copy(wu_hbm.at[0], wgu.at[:, pl.ds(HIDDEN, HIDDEN)], wsem.at[5]),
        pltpu.make_async_copy(wd_hbm.at[0], wd, wsem.at[6]),
    ]

    def cache_copies(t):
        m = lax.rem(s + TURNS - t, TURNS)
        copies = []
        for g in range(2):
            copies.append(
                pltpu.make_async_copy(kc_hbm.at[0, m, :, g], kc.at[t, g], csem.at[t, g])
            )
            copies.append(
                pltpu.make_async_copy(vc_hbm.at[0, m, :, g], vc.at[t, g], csem.at[t, 2 + g])
            )
        return copies

    for copy in weight_copies[:3]:
        copy.start()
    for copy in cache_copies(0):
        copy.start()
    for copy in weight_copies[3:]:
        copy.start()
    for t in range(1, TURNS):
        for copy in cache_copies(t):
            copy.start()

    barrier = pltpu.get_barrier_semaphore()

    def greet(i, _):
        other = lax.rem(me + i, GROUP)
        pl.semaphore_signal(
            barrier,
            inc=1,
            device_id=(s, other // COLS, lax.rem(other, COLS)),
            device_id_type=pl.DeviceIdType.MESH,
        )
        return 0

    lax.fori_loop(1, GROUP, greet, 0)
    for i in range(COLS):
        pl.semaphore_signal(
            barrier, inc=1, device_id=(s_prev, r, i), device_id_type=pl.DeviceIdType.MESH
        )

    init[c] = jnp.zeros((80, 256), bf16)
    init[c, 0:64, 0:PIECE] = hid_ref[0]
    gain_row = lax.broadcasted_iota(jnp.int32, (SUB, PIECE), 0)
    init[c, 64:80, 0:PIECE] = jnp.where(
        gain_row == 0, ag_ref[...].astype(f32), fg_ref[...].astype(f32)
    ).astype(bf16)

    stream_row = lax.broadcasted_iota(jnp.int32, (LOCAL, LOCAL * CTX), 0)
    position = lax.broadcasted_iota(jnp.int32, (LOCAL, LOCAL * CTX), 1)
    for t in range(TURNS):
        m = lax.rem(s + TURNS - t, TURNS)
        offsets = jnp.full((LOCAL, LOCAL * CTX), masked_score, f32)
        for b in range(LOCAL):
            live = (
                (stream_row == b)
                & (position >= b * CTX)
                & (position < b * CTX + len_ref[m, b])
            )
            offsets = jnp.where(live, 0.0, offsets)
        bias[t] = offsets

    pl.semaphore_wait(barrier, GROUP - 1 + COLS)

    def send_init(i):
        return remote(
            init.at[c], init.at[c], send0.at[i], recv0.at[c], (s, r, col_at(i))
        )

    def wait_init(i):
        return remote(
            init.at[col_at(i)], init.at[col_at(i)], send0.at[i], recv0.at[col_at(i)],
            (s, r, col_at(i)),
        )

    for i in range(1, COLS):
        send_init(i).start()
    for i in range(1, COLS):
        wait_init(i).wait_recv()
    joined = None
    for i in range(COLS):
        piece = jnp.concatenate(
            [init[i].astype(f32), jnp.zeros((80, WIDE - 256), f32)], axis=1
        )
        if i:
            piece = pltpu.roll(piece, i * PIECE, 1)
        joined = piece if joined is None else joined + piece
    xin[0] = joined[0:64].astype(bf16).reshape(COLS, SUB, WIDE)
    gain1[...] = joined[64:65]
    gain2[r] = jnp.broadcast_to(joined[65:66], (8, WIDE))

    def send_gain(i):
        return remote(
            gain2.at[r], gain2.at[r], sendg.at[i], recvg.at[r], (s, row_at(i), c)
        )

    def wait_gain(i):
        return remote(
            gain2.at[row_at(i)], gain2.at[row_at(i)], sendg.at[i], recvg.at[row_at(i)],
            (s, row_at(i), c),
        )

    def turn(t, _):
        x_all = xin[t].reshape(STREAMS, WIDE).astype(f32)
        squares = jnp.sum(x_all * x_all, axis=1, keepdims=True)
        high = squares.astype(bf16).astype(f32)
        low = squares - high
        left = (x_all * gain1[...]).astype(bf16)

        @pl.when(t == 0)
        def _():
            for copy in weight_copies[:3]:
                copy.wait()

        part = jnp.dot(left, wqkv[...], preferred_element_type=f32)
        part = part.reshape(ROWS, LOCAL, QKV)
        s2[:, :, 0:HALF] = jnp.concatenate(
            [part[:, :, 0:HALF], part[:, :, HALF:QKV]], axis=1
        ).astype(bf16)
        s2[:, :, HALF:1024] = jnp.broadcast_to(
            jnp.concatenate(
                [high.reshape(ROWS, LOCAL, 1), low.reshape(ROWS, LOCAL, 1)], axis=1
            ),
            (ROWS, SUB, 128),
        ).astype(bf16)

        def send_two(i):
            return remote(
                s2.at[row_at(i)], r2.at[r], send2.at[i], recv2.at[r], (s, row_at(i), c)
            )

        def wait_two(i):
            return remote(
                s2.at[row_at(i)], r2.at[row_at(i)], send2.at[i], recv2.at[row_at(i)],
                (s, row_at(i), c),
            )

        for i in (4, 3, 5, 2, 6, 1, 7):
            send_two(i).start()

        @pl.when(t == 0)
        def _():
            for i in range(1, ROWS):
                send_gain(i).start()

        total = s2[r].astype(f32)
        for i in (1, 7, 2, 6, 3, 5, 4):
            wait_two(i).wait_recv()
            total = total + r2[row_at(i)].astype(f32)
        mean_square = (total[0:8, HALF:HALF + 1] + total[8:16, HALF:HALF + 1]) / D
        scale = lax.rsqrt(mean_square + norm_eps)
        top = (total[0:8, 0:HALF] * scale).astype(bf16).astype(f32)
        bottom = (total[8:16, 0:HALF] * scale).astype(bf16).astype(f32)

        def head(j):
            if j < 7:
                return top[:, j * HD:(j + 1) * HD]
            return bottom[:, (j - 7) * HD:(j - 6) * HD]

        @pl.when(t == 0)
        def _():
            for copy in cache_copies(0):
                copy.wait()

        @pl.when(t > 0)
        def _():
            for copy in cache_copies(t):
                copy.wait()

        score_scale = 1.0 / math.sqrt(HD)
        offsets = jnp.concatenate([bias[t]] * 5, axis=0)
        mixed_rows = []
        for g in range(2):
            queries = jnp.concatenate([head(5 * g + j) for j in range(5)], axis=0)
            key_new = jnp.concatenate([head(10 + g)] * 5, axis=0)
            value_new = jnp.concatenate([head(12 + g)] * 5, axis=0)
            keys = kc[t, g].reshape(LOCAL * CTX, HD)
            values = vc[t, g].reshape(LOCAL * CTX, HD)
            scores = lax.dot_general(
                queries.astype(bf16), keys, (((1,), (1,)), ((), ())),
                preferred_element_type=f32,
            )
            scores = scores * score_scale + offsets
            self_score = jnp.sum(queries * key_new, axis=1, keepdims=True) * score_scale
            row_max = jnp.maximum(jnp.max(scores, axis=1, keepdims=True), self_score)
            weights = jnp.exp(scores - row_max)
            self_weight = jnp.exp(self_score - row_max)
            denominator = jnp.sum(weights, axis=1, keepdims=True) + self_weight
            probs = (weights / denominator).astype(bf16)
            self_prob = (self_weight / denominator).astype(bf16).astype(f32)
            mixed = jnp.dot(probs, values, preferred_element_type=f32)
            mixed = mixed + self_prob * value_new
            mixed_rows.append(
                jnp.concatenate([mixed[j * 8:(j + 1) * 8] for j in range(5)], axis=1)
            )
        o3[r] = jnp.concatenate(mixed_rows, axis=0).astype(bf16)

        def send_three(i):
            return remote(
                o3.at[r], o3.at[r], send3.at[i], recv3.at[r], (s, row_at(i), c)
            )

        def wait_three(i):
            return remote(
                o3.at[row_at(i)], o3.at[row_at(i)], send3.at[i], recv3.at[row_at(i)],
                (s, row_at(i), c),
            )

        for i in (4, 3, 5, 2, 6, 1, 7):
            send_three(i).start()

        @pl.when(t == 0)
        def _():
            weight_copies[3].wait()

        for i in (1, 7, 2, 6, 3, 5, 4):
            wait_three(i).wait_recv()
        gathered = o3[...].astype(f32)
        heads = jnp.concatenate(
            [gathered[:, 0:8].reshape(STREAMS, WIDE), gathered[:, 8:16].reshape(STREAMS, WIDE)],
            axis=1,
        ).astype(bf16)
        out_part = jnp.dot(heads, wo[...], preferred_element_type=f32)
        s4[...] = out_part.astype(bf16).reshape(COLS, SUB, WIDE)

        def send_four(i):
            return remote(
                s4.at[col_at(i)], r4.at[c], send4.at[i], recv4.at[c], (s, r, col_at(i))
            )

        def wait_four(i):
            return remote(
                s4.at[col_at(i)], r4.at[col_at(i)], send4.at[i], recv4.at[col_at(i)],
                (s, r, col_at(i)),
            )

        for i in (2, 1, 3):
            send_four(i).start()
        after = xin[t, c].astype(f32) + s4[c].astype(f32)
        for i in (1, 3, 2):
            wait_four(i).wait_recv()
            after = after + r4[col_at(i)].astype(f32)
        x2_all[r, c] = after.astype(bf16)
        after = x2_all[r, c].astype(f32)

        def send_five(i, _):
            other = lax.rem(me + i, GROUP)
            remote(
                x2_all.at[r, c], x2_all.at[r, c], send5.at[i], recv5.at[me],
                (s, other // COLS, lax.rem(other, COLS)),
            ).start()
            return 0

        lax.fori_loop(1, GROUP, send_five, 0)

        @pl.when(t == 0)
        def _():
            for i in range(1, ROWS):
                wait_gain(i).wait_recv()
            for copy in weight_copies[4:6]:
                copy.wait()

        acc[...] = jnp.zeros_like(acc)

        def chip_at(j):
            return lax.rem(x_chip + j + (j // 2) * (5 - 2 * j), 4)

        def gate_step(j, squares):
            xc = chip_at(j)
            for k in range(2):
                for q in range(COLS):
                    row = 2 * xc + k
                    src = row * COLS + q

                    @pl.when(src != me)
                    def _():
                        remote(
                            x2_all.at[row, q], x2_all.at[row, q], send5.at[0],
                            recv5.at[src], (s, row, q),
                        ).wait_recv()

            values = jnp.concatenate(
                [x2_all[2 * xc + k].reshape(STREAMS, WIDE) for k in range(2)], axis=1
            ).astype(f32)
            gains = jnp.concatenate([gain2[2 * xc + k, 0:1] for k in range(2)], axis=1)
            square = values * values
            for k in range(10):
                squares = squares + square[:, k * 128:(k + 1) * 128]
            scaled = (values * gains).astype(bf16)
            first = pl.multiple_of(xc * 1280, 1280)
            acc[...] += jnp.dot(
                scaled, wgu[pl.ds(first, 1280), :], preferred_element_type=f32
            )
            return squares

        squares = lax.fori_loop(0, 4, gate_step, jnp.zeros((STREAMS, 128), f32))
        mean_square = jnp.sum(squares, axis=1, keepdims=True) / D
        scale = lax.rsqrt(mean_square + norm_eps)
        gate = acc[:, 0:HIDDEN] * scale
        up = acc[:, HIDDEN:2 * HIDDEN] * scale
        activation = (gate / (1.0 + jnp.exp(-gate)) * up).astype(bf16)

        @pl.when(t == 0)
        def _():
            weight_copies[6].wait()

        def down_step(j, _):
            xc = chip_at(3 - j)
            first = pl.multiple_of(xc * 1280, 1280)
            part = jnp.dot(
                activation, wd[:, pl.ds(first, 1280)], preferred_element_type=f32
            ).astype(bf16)
            for k in range(2):
                s6[2 * xc + k] = part[:, k * WIDE:(k + 1) * WIDE].reshape(COLS, SUB, WIDE)
            for k in range(2):
                for q in range(COLS):
                    row = 2 * xc + k
                    dst = row * COLS + q

                    @pl.when(dst != me)
                    def _():
                        remote(
                            s6.at[row, q], r6.at[r, c], send6.at[dst], recv6.at[me],
                            (s, row, q),
                        ).start()

            return 0

        lax.fori_loop(0, 4, down_step, 0)

        def sum_six(i, total):
            other = lax.rem(me + i, GROUP)
            row, q = other // COLS, lax.rem(other, COLS)
            remote(
                s6.at[row, q], r6.at[row, q], send6.at[other], recv6.at[other], (s, row, q)
            ).wait_recv()
            return total + r6[row, q].astype(f32)

        total = lax.fori_loop(1, GROUP, sum_six, after + s6[r, c].astype(f32))
        x_send[...] = total.astype(bf16)

        def send_one(i):
            return remote(
                x_send, xin.at[t + 1, c], send1.at[i], recv1.at[t, c],
                (s_next, r, col_at(i)),
            )

        def wait_one(i):
            return remote(
                x_send, xin.at[t + 1, col_at(i)], send1.at[i], recv1.at[t, col_at(i)],
                (s_next, r, col_at(i)),
            )

        for i in range(COLS):
            send_one(i).start()

        for i in range(1, ROWS):
            send_two(i).wait_send()
            send_three(i).wait_send()
        for i in range(1, COLS):
            send_four(i).wait_send()

        def finish(i, _):
            other = lax.rem(me + i, GROUP)
            row, q = other // COLS, lax.rem(other, COLS)
            remote(
                x2_all.at[r, c], x2_all.at[r, c], send5.at[i], recv5.at[me], (s, row, q)
            ).wait_send()
            remote(
                s6.at[row, q], r6.at[r, c], send6.at[other], recv6.at[me], (s, row, q)
            ).wait_send()
            return 0

        lax.fori_loop(1, GROUP, finish, 0)
        for i in range(COLS):
            send_one(i).wait_send()
        for i in range(COLS):
            wait_one(i).wait_recv()
        return 0

    lax.fori_loop(0, TURNS, turn, 0)

    final = xin[TURNS].reshape(STREAMS, WIDE).astype(f32)
    final = pltpu.roll(final, lax.rem(WIDE - c * PIECE, WIDE), 1)
    out_ref[0] = final[:, 0:PIECE].astype(bf16)
    for i in range(1, COLS):
        send_init(i).wait_send()
    for i in range(1, ROWS):
        send_gain(i).wait_send()


def per_device(
    hidden,
    lengths,
    attn_gain,
    ffn_gain,
    q_weight,
    key_weight,
    value_weight,
    out_weight,
    gate_weight,
    up_weight,
    down_weight,
    key_cache,
    value_cache,
):
    vmem = pl.BlockSpec(memory_space=pltpu.VMEM)
    hbm = pl.BlockSpec(memory_space=pl.ANY)
    dma = pltpu.SemaphoreType.DMA
    return pl.pallas_call(
        kernel,
        out_shape=jax.ShapeDtypeStruct((1, STREAMS, PIECE), bf16),
        in_specs=[pl.BlockSpec(memory_space=pltpu.SMEM), vmem, vmem, vmem] + [hbm] * 9,
        out_specs=vmem,
        scratch_shapes=[
            pltpu.VMEM((WIDE, QKV), bf16),
            pltpu.VMEM((1280, WIDE), bf16),
            pltpu.VMEM((D, 2 * HIDDEN), bf16),
            pltpu.VMEM((HIDDEN, D), bf16),
            pltpu.VMEM((TURNS, 2, LOCAL, CTX, HD), bf16),
            pltpu.VMEM((TURNS, 2, LOCAL, CTX, HD), bf16),
            pltpu.VMEM((COLS, 80, 256), bf16),
            pltpu.VMEM((1, WIDE), f32),
            pltpu.VMEM((ROWS, 8, WIDE), f32),
            pltpu.VMEM((TURNS, LOCAL, LOCAL * CTX), f32),
            pltpu.VMEM((TURNS + 1, COLS, SUB, WIDE), bf16),
            pltpu.VMEM((ROWS, SUB, 1024), bf16),
            pltpu.VMEM((ROWS, SUB, 1024), bf16),
            pltpu.VMEM((ROWS, SUB, WIDE), bf16),
            pltpu.VMEM((COLS, SUB, WIDE), bf16),
            pltpu.VMEM((COLS, SUB, WIDE), bf16),
            pltpu.VMEM((ROWS, COLS, SUB, WIDE), bf16),
            pltpu.VMEM((STREAMS, 2 * HIDDEN), f32),
            pltpu.VMEM((ROWS, COLS, SUB, WIDE), bf16),
            pltpu.VMEM((ROWS, COLS, SUB, WIDE), bf16),
            pltpu.VMEM((SUB, WIDE), bf16),
            dma((7,)),
            dma((TURNS, 4)),
            dma((COLS,)),
            dma((COLS,)),
            dma((ROWS,)),
            dma((ROWS,)),
            dma((COLS,)),
            dma((TURNS, COLS)),
            dma((ROWS,)),
            dma((ROWS,)),
            dma((ROWS,)),
            dma((ROWS,)),
            dma((COLS,)),
            dma((COLS,)),
            dma((GROUP,)),
            dma((GROUP,)),
            dma((GROUP,)),
            dma((GROUP,)),
        ],
        compiler_params=pltpu.CompilerParams(
            collective_id=0, has_side_effects=True, vmem_limit_bytes=56 * 1024 * 1024
        ),
        cost_estimate=pl.CostEstimate(
            flops=TURNS * 2 * STREAMS * 9830400, bytes_accessed=24_000_000, transcendentals=0
        ),
    )(
        lengths,
        hidden,
        attn_gain,
        ffn_gain,
        q_weight,
        key_weight,
        value_weight,
        out_weight,
        gate_weight,
        up_weight,
        down_weight,
        key_cache,
        value_cache,
    )


def solution(mesh):
    return jax.shard_map(
        per_device,
        mesh=mesh,
        in_specs=(
            P("section", None, ("row", "col")),
            P(None, "row"),
            P("section", ("row", "col")),
            P("section", ("row", "col")),
            P("section", "row", "col"),
            P("section", "row", "col"),
            P("section", "row", "col"),
            P("section", "col", "row"),
            P("section", None, ("row", "col")),
            P("section", None, ("row", "col")),
            P("section", ("row", "col"), None),
            P("section", None, "row", "col", None, None),
            P("section", None, "row", "col", None, None),
        ),
        out_specs=P("section", None, ("row", "col")),
        check_vma=False,
    )
```

```python
import functools
import math

import jax
import jax.numpy as jnp
from jax import lax
from jax.experimental import pallas as pl
from jax.experimental.pallas import tpu as pltpu
from jax.sharding import PartitionSpec as P

D = 5120
HD = 128
CTX = 96
TURNS = 4
ROWS = 8
COLS = 4
CHIPS = 4
PEERS = 16
WIDE = 640
PIECE = 160
SUB = 16
STREAMS = 64
LOCAL = 8
QKV = 1792
HALF = 896
HIDDEN = 512
norm_eps = 1e-06
masked_score = -1e30
f32 = jnp.float32
bf16 = jnp.bfloat16


def remote(src, dst, send, recv, device):
    return pltpu.make_async_remote_copy(
        src_ref=src,
        dst_ref=dst,
        send_sem=send,
        recv_sem=recv,
        device_id=device,
        device_id_type=pl.DeviceIdType.MESH,
    )


def kernel(
    len_ref,
    hid_ref,
    ag_ref,
    fg_ref,
    wq_hbm,
    wk_hbm,
    wv_hbm,
    wo_hbm,
    wg_hbm,
    wu_hbm,
    wd_hbm,
    kc_hbm,
    vc_hbm,
    out_ref,
    wqkv,
    wo,
    wgu,
    wd,
    kc,
    vc,
    init,
    gain1,
    gain2,
    bias,
    xin,
    s2,
    r2,
    o3,
    s4,
    r4,
    x2_all,
    acc,
    keep,
    p6,
    q6,
    s6,
    r6,
    x_send,
    wsem,
    csem,
    send0,
    recv0,
    sendg,
    recvg,
    send1,
    recv1,
    send2,
    recv2,
    send3,
    recv3,
    send4,
    recv4,
    send5,
    recv5,
    send_f,
    recv_f,
    send_p,
    recv_p,
    send6,
    recv6,
):
    s = lax.axis_index("section")
    r = lax.axis_index("row")
    c = lax.axis_index("col")
    x_chip = r // 2
    core = lax.rem(r, 2)
    pair = 2 * x_chip + 1 - core
    s_next = lax.rem(s + 1, TURNS)
    s_prev = lax.rem(s + TURNS - 1, TURNS)

    def row_at(i):
        return lax.rem(r + i, ROWS)

    def col_at(i):
        return lax.rem(c + i, COLS)

    weight_copies = [
        pltpu.make_async_copy(wq_hbm.at[0], wqkv.at[:, pl.ds(0, 1280)], wsem.at[0]),
        pltpu.make_async_copy(wk_hbm.at[0], wqkv.at[:, pl.ds(1280, 256)], wsem.at[1]),
        pltpu.make_async_copy(wv_hbm.at[0], wqkv.at[:, pl.ds(1536, 256)], wsem.at[2]),
        pltpu.make_async_copy(wo_hbm.at[0], wo, wsem.at[3]),
        pltpu.make_async_copy(wg_hbm.at[0], wgu.at[:, pl.ds(0, HIDDEN)], wsem.at[4]),
        pltpu.make_async_copy(wu_hbm.at[0], wgu.at[:, pl.ds(HIDDEN, HIDDEN)], wsem.at[5]),
        pltpu.make_async_copy(wd_hbm.at[0], wd, wsem.at[6]),
    ]

    def cache_copies(t):
        m = lax.rem(s + TURNS - t, TURNS)
        copies = []
        for g in range(2):
            copies.append(
                pltpu.make_async_copy(kc_hbm.at[0, m, :, g], kc.at[t, g], csem.at[t, g])
            )
            copies.append(
                pltpu.make_async_copy(vc_hbm.at[0, m, :, g], vc.at[t, g], csem.at[t, 2 + g])
            )
        return copies

    for copy in weight_copies[:3]:
        copy.start()
    for copy in cache_copies(0):
        copy.start()
    for copy in weight_copies[3:]:
        copy.start()
    for t in range(1, TURNS):
        for copy in cache_copies(t):
            copy.start()

    barrier = pltpu.get_barrier_semaphore()

    def row_of(dx):
        return 2 * lax.rem(x_chip + dx, CHIPS) + core

    greeted = [(s, row_of(i // COLS), col_at(i % COLS)) for i in range(1, PEERS)]
    greeted += [(s, 2 * lax.rem(x_chip + i, CHIPS) + 1 - core, c) for i in range(CHIPS)]
    greeted += [(s_prev, r, i) for i in range(COLS)]
    for device in greeted:
        pl.semaphore_signal(
            barrier, inc=1, device_id=device, device_id_type=pl.DeviceIdType.MESH
        )

    init[c] = jnp.zeros((80, 256), bf16)
    init[c, 0:64, 0:PIECE] = hid_ref[0]
    gain_row = lax.broadcasted_iota(jnp.int32, (SUB, PIECE), 0)
    init[c, 64:80, 0:PIECE] = jnp.where(
        gain_row == 0, ag_ref[...].astype(f32), fg_ref[...].astype(f32)
    ).astype(bf16)

    stream_row = lax.broadcasted_iota(jnp.int32, (LOCAL, LOCAL * CTX), 0)
    position = lax.broadcasted_iota(jnp.int32, (LOCAL, LOCAL * CTX), 1)
    for t in range(TURNS):
        m = lax.rem(s + TURNS - t, TURNS)
        offsets = jnp.full((LOCAL, LOCAL * CTX), masked_score, f32)
        for b in range(LOCAL):
            live = (
                (stream_row == b)
                & (position >= b * CTX)
                & (position < b * CTX + len_ref[m, b])
            )
            offsets = jnp.where(live, 0.0, offsets)
        bias[t] = offsets

    pl.semaphore_wait(barrier, len(greeted))

    def send_init(i):
        return remote(
            init.at[c], init.at[c], send0.at[i], recv0.at[c], (s, r, col_at(i))
        )

    def wait_init(i):
        return remote(
            init.at[col_at(i)], init.at[col_at(i)], send0.at[i], recv0.at[col_at(i)],
            (s, r, col_at(i)),
        )

    for i in range(1, COLS):
        send_init(i).start()
    for i in range(1, COLS):
        wait_init(i).wait_recv()
    joined = None
    for i in range(COLS):
        piece = jnp.concatenate(
            [init[i].astype(f32), jnp.zeros((80, WIDE - 256), f32)], axis=1
        )
        if i:
            piece = pltpu.roll(piece, i * PIECE, 1)
        joined = piece if joined is None else joined + piece
    xin[0] = joined[0:64].astype(bf16).reshape(COLS, SUB, WIDE)
    gain1[...] = joined[64:65]
    gain2[r] = jnp.broadcast_to(joined[65:66], (8, WIDE))

    def send_gain(i):
        return remote(
            gain2.at[r], gain2.at[r], sendg.at[i], recvg.at[r], (s, row_at(i), c)
        )

    def wait_gain(i):
        return remote(
            gain2.at[row_at(i)], gain2.at[row_at(i)], sendg.at[i], recvg.at[row_at(i)],
            (s, row_at(i), c),
        )

    def turn(t, _):
        x_all = xin[t].reshape(STREAMS, WIDE).astype(f32)
        squares = jnp.sum(x_all * x_all, axis=1, keepdims=True)
        high = squares.astype(bf16).astype(f32)
        low = squares - high
        left = (x_all * gain1[...]).astype(bf16)

        @pl.when(t == 0)
        def _():
            for copy in weight_copies[:3]:
                copy.wait()

        part = jnp.dot(left, wqkv[...], preferred_element_type=f32)
        part = part.reshape(ROWS, LOCAL, QKV)
        s2[:, :, 0:HALF] = jnp.concatenate(
            [part[:, :, 0:HALF], part[:, :, HALF:QKV]], axis=1
        ).astype(bf16)
        s2[:, :, HALF:1024] = jnp.broadcast_to(
            jnp.concatenate(
                [high.reshape(ROWS, LOCAL, 1), low.reshape(ROWS, LOCAL, 1)], axis=1
            ),
            (ROWS, SUB, 128),
        ).astype(bf16)

        def send_two(i):
            return remote(
                s2.at[row_at(i)], r2.at[r], send2.at[i], recv2.at[r], (s, row_at(i), c)
            )

        def wait_two(i):
            return remote(
                s2.at[row_at(i)], r2.at[row_at(i)], send2.at[i], recv2.at[row_at(i)],
                (s, row_at(i), c),
            )

        for i in (4, 3, 5, 2, 6, 1, 7):
            send_two(i).start()

        @pl.when(t == 0)
        def _():
            for i in range(1, ROWS):
                send_gain(i).start()

        total = s2[r].astype(f32)
        for i in (1, 7, 2, 6, 3, 5, 4):
            wait_two(i).wait_recv()
            total = total + r2[row_at(i)].astype(f32)
        mean_square = (total[0:8, HALF:HALF + 1] + total[8:16, HALF:HALF + 1]) / D
        scale = lax.rsqrt(mean_square + norm_eps)
        top = (total[0:8, 0:HALF] * scale).astype(bf16).astype(f32)
        bottom = (total[8:16, 0:HALF] * scale).astype(bf16).astype(f32)

        def head(j):
            if j < 7:
                return top[:, j * HD:(j + 1) * HD]
            return bottom[:, (j - 7) * HD:(j - 6) * HD]

        @pl.when(t == 0)
        def _():
            for copy in cache_copies(0):
                copy.wait()

        @pl.when(t > 0)
        def _():
            for copy in cache_copies(t):
                copy.wait()

        score_scale = 1.0 / math.sqrt(HD)
        offsets = jnp.concatenate([bias[t]] * 5, axis=0)
        mixed_rows = []
        for g in range(2):
            queries = jnp.concatenate([head(5 * g + j) for j in range(5)], axis=0)
            key_new = jnp.concatenate([head(10 + g)] * 5, axis=0)
            value_new = jnp.concatenate([head(12 + g)] * 5, axis=0)
            keys = kc[t, g].reshape(LOCAL * CTX, HD)
            values = vc[t, g].reshape(LOCAL * CTX, HD)
            scores = lax.dot_general(
                queries.astype(bf16), keys, (((1,), (1,)), ((), ())),
                preferred_element_type=f32,
            )
            scores = scores * score_scale + offsets
            self_score = jnp.sum(queries * key_new, axis=1, keepdims=True) * score_scale
            row_max = jnp.maximum(jnp.max(scores, axis=1, keepdims=True), self_score)
            weights = jnp.exp(scores - row_max)
            self_weight = jnp.exp(self_score - row_max)
            denominator = jnp.sum(weights, axis=1, keepdims=True) + self_weight
            probs = (weights / denominator).astype(bf16)
            self_prob = (self_weight / denominator).astype(bf16).astype(f32)
            mixed = jnp.dot(probs, values, preferred_element_type=f32)
            mixed = mixed + self_prob * value_new
            mixed_rows.append(
                jnp.concatenate([mixed[j * 8:(j + 1) * 8] for j in range(5)], axis=1)
            )
        o3[r] = jnp.concatenate(mixed_rows, axis=0).astype(bf16)

        def send_three(i):
            return remote(
                o3.at[r], o3.at[r], send3.at[i], recv3.at[r], (s, row_at(i), c)
            )

        def wait_three(i):
            return remote(
                o3.at[row_at(i)], o3.at[row_at(i)], send3.at[i], recv3.at[row_at(i)],
                (s, row_at(i), c),
            )

        for i in (4, 3, 5, 2, 6, 1, 7):
            send_three(i).start()

        @pl.when(t == 0)
        def _():
            weight_copies[3].wait()

        for i in (1, 7, 2, 6, 3, 5, 4):
            wait_three(i).wait_recv()
        gathered = o3[...].astype(f32)
        heads = jnp.concatenate(
            [gathered[:, 0:8].reshape(STREAMS, WIDE), gathered[:, 8:16].reshape(STREAMS, WIDE)],
            axis=1,
        ).astype(bf16)
        out_part = jnp.dot(heads, wo[...], preferred_element_type=f32)
        s4[...] = out_part.astype(bf16).reshape(COLS, SUB, WIDE)

        def send_four(i):
            return remote(
                s4.at[col_at(i)], r4.at[c], send4.at[i], recv4.at[c], (s, r, col_at(i))
            )

        def wait_four(i):
            return remote(
                s4.at[col_at(i)], r4.at[col_at(i)], send4.at[i], recv4.at[col_at(i)],
                (s, r, col_at(i)),
            )

        for i in (2, 1, 3):
            send_four(i).start()
        after = xin[t, c].astype(f32) + s4[c].astype(f32)
        for i in (1, 3, 2):
            wait_four(i).wait_recv()
            after = after + r4[col_at(i)].astype(f32)
        x2_all[r, c] = after.astype(bf16)
        after = x2_all[r, c].astype(f32)

        def send_five(i):
            return remote(
                x2_all.at[r, c], x2_all.at[r, c], send5.at[i], recv5.at[x_chip, c],
                (s, row_of(i // COLS), col_at(i % COLS)),
            )

        for i in (2, 1, 3, 6, 14, 5, 7, 13, 15, 4, 12, 10, 9, 11, 8):
            send_five(i).start()

        @pl.when(t == 0)
        def _():
            for i in range(1, ROWS):
                wait_gain(i).wait_recv()
            for copy in weight_copies[4:6]:
                copy.wait()

        acc[...] = jnp.zeros_like(acc)

        def chip_at(j):
            return lax.rem(x_chip + j + (j // 2) * (5 - 2 * j), 4)

        def forward(xc):
            row = 2 * xc + core
            return remote(
                x2_all.at[row], x2_all.at[row], send_f.at[xc], recv_f.at[xc], (s, pair, c)
            )

        def collect(j):
            xc = chip_at(j)
            for q in range(COLS):

                @pl.when((xc != x_chip) | (q != c))
                def _():
                    row = 2 * xc + core
                    remote(
                        x2_all.at[row, q], x2_all.at[row, q], send5.at[0],
                        recv5.at[xc, q], (s, pair, c),
                    ).wait_recv()

            forward(xc).start()

        def gate_step(j, squares):
            @pl.when(j < CHIPS - 1)
            def _():
                collect(j + 1)

            xc = chip_at(j)
            row = 2 * xc + 1 - core
            remote(
                x2_all.at[row], x2_all.at[row], send_f.at[xc], recv_f.at[xc], (s, pair, c)
            ).wait_recv()
            values = jnp.concatenate(
                [x2_all[2 * xc + k].reshape(STREAMS, WIDE) for k in range(2)], axis=1
            ).astype(f32)
            gains = jnp.concatenate([gain2[2 * xc + k, 0:1] for k in range(2)], axis=1)
            square = values * values
            for k in range(10):
                squares = squares + square[:, k * 128:(k + 1) * 128]
            scaled = (values * gains).astype(bf16)
            first = pl.multiple_of(xc * 1280, 1280)
            acc[...] += jnp.dot(
                scaled, wgu[pl.ds(first, 1280), :], preferred_element_type=f32
            )
            return squares

        collect(0)
        squares = lax.fori_loop(0, CHIPS, gate_step, jnp.zeros((STREAMS, 128), f32))
        mean_square = jnp.sum(squares, axis=1, keepdims=True) / D
        scale = lax.rsqrt(mean_square + norm_eps)
        gate = acc[:, 0:HIDDEN] * scale
        up = acc[:, HIDDEN:2 * HIDDEN] * scale
        activation = (gate / (1.0 + jnp.exp(-gate)) * up).astype(bf16)

        @pl.when(t == 0)
        def _():
            weight_copies[6].wait()

        def swap(xc):
            return remote(
                p6.at[xc], q6.at[xc], send_p.at[xc], recv_p.at[xc], (s, pair, c)
            )

        def down_step(j, _):
            xc = chip_at(CHIPS - 1 - j)
            first = pl.multiple_of(xc * 1280, 1280)
            part = jnp.dot(
                activation, wd[:, pl.ds(first, 1280)], preferred_element_type=f32
            )
            lower, upper = part[:, 0:WIDE], part[:, WIDE:1280]
            keep[xc] = jnp.where(core == 0, lower, upper)
            p6[xc] = jnp.where(core == 0, upper, lower).astype(bf16)
            swap(xc).start()
            return 0

        lax.fori_loop(0, CHIPS, down_step, 0)

        def send_six(xc, i):
            q = col_at(i)
            return remote(
                s6.at[xc, q], r6.at[x_chip, c], send6.at[xc, i], recv6.at[x_chip, c],
                (s, 2 * xc + core, q),
            )

        def share_step(j, _):
            xc = chip_at(CHIPS - 1 - j)
            swap(xc).wait_recv()
            both = keep[xc] + q6[xc].astype(f32)
            s6[xc] = both.astype(bf16).reshape(COLS, SUB, WIDE)
            for i in (2, 1, 3):
                send_six(xc, i).start()

            @pl.when(xc != x_chip)
            def _():
                send_six(xc, 0).start()

            return 0

        lax.fori_loop(0, CHIPS, share_step, 0)

        def sum_step(j, total):
            xc = chip_at(j)
            for i in (1, 3, 2):
                q = col_at(i)
                remote(
                    s6.at[xc, q], r6.at[xc, q], send6.at[xc, i], recv6.at[xc, q],
                    (s, pair, c),
                ).wait_recv()
                total = total + r6[xc, q].astype(f32)
            return total

        total = sum_step(0, after + s6[x_chip, c].astype(f32))

        def far_step(j, total):
            xc = chip_at(j)
            remote(
                s6.at[xc, c], r6.at[xc, c], send6.at[xc, 0], recv6.at[xc, c], (s, pair, c)
            ).wait_recv()
            return sum_step(j, total + r6[xc, c].astype(f32))

        total = lax.fori_loop(1, CHIPS, far_step, total)
        x_send[...] = total.astype(bf16)

        def send_one(i):
            return remote(
                x_send, xin.at[t + 1, c], send1.at[i], recv1.at[t, c],
                (s_next, r, col_at(i)),
            )

        def wait_one(i):
            return remote(
                x_send, xin.at[t + 1, col_at(i)], send1.at[i], recv1.at[t, col_at(i)],
                (s_next, r, col_at(i)),
            )

        for i in range(COLS):
            send_one(i).start()

        for i in range(1, ROWS):
            send_two(i).wait_send()
            send_three(i).wait_send()
        for i in range(1, COLS):
            send_four(i).wait_send()

        for i in range(1, PEERS):
            send_five(i).wait_send()
        for i in range(CHIPS):
            forward(i).wait_send()
            swap(i).wait_send()
            for k in range(1, COLS):
                send_six(i, k).wait_send()

            @pl.when(i != x_chip)
            def _():
                send_six(i, 0).wait_send()

        for i in range(COLS):
            send_one(i).wait_send()
        for i in range(COLS):
            wait_one(i).wait_recv()
        return 0

    lax.fori_loop(0, TURNS, turn, 0)

    final = xin[TURNS].reshape(STREAMS, WIDE).astype(f32)
    final = pltpu.roll(final, lax.rem(WIDE - c * PIECE, WIDE), 1)
    out_ref[0] = final[:, 0:PIECE].astype(bf16)
    for i in range(1, COLS):
        send_init(i).wait_send()
    for i in range(1, ROWS):
        send_gain(i).wait_send()


def per_device(
    hidden,
    lengths,
    attn_gain,
    ffn_gain,
    q_weight,
    key_weight,
    value_weight,
    out_weight,
    gate_weight,
    up_weight,
    down_weight,
    key_cache,
    value_cache,
):
    vmem = pl.BlockSpec(memory_space=pltpu.VMEM)
    hbm = pl.BlockSpec(memory_space=pl.ANY)
    dma = pltpu.SemaphoreType.DMA
    return pl.pallas_call(
        kernel,
        out_shape=jax.ShapeDtypeStruct((1, STREAMS, PIECE), bf16),
        in_specs=[pl.BlockSpec(memory_space=pltpu.SMEM), vmem, vmem, vmem] + [hbm] * 9,
        out_specs=vmem,
        scratch_shapes=[
            pltpu.VMEM((WIDE, QKV), bf16),
            pltpu.VMEM((1280, WIDE), bf16),
            pltpu.VMEM((D, 2 * HIDDEN), bf16),
            pltpu.VMEM((HIDDEN, D), bf16),
            pltpu.VMEM((TURNS, 2, LOCAL, CTX, HD), bf16),
            pltpu.VMEM((TURNS, 2, LOCAL, CTX, HD), bf16),
            pltpu.VMEM((COLS, 80, 256), bf16),
            pltpu.VMEM((1, WIDE), f32),
            pltpu.VMEM((ROWS, 8, WIDE), f32),
            pltpu.VMEM((TURNS, LOCAL, LOCAL * CTX), f32),
            pltpu.VMEM((TURNS + 1, COLS, SUB, WIDE), bf16),
            pltpu.VMEM((ROWS, SUB, 1024), bf16),
            pltpu.VMEM((ROWS, SUB, 1024), bf16),
            pltpu.VMEM((ROWS, SUB, WIDE), bf16),
            pltpu.VMEM((COLS, SUB, WIDE), bf16),
            pltpu.VMEM((COLS, SUB, WIDE), bf16),
            pltpu.VMEM((ROWS, COLS, SUB, WIDE), bf16),
            pltpu.VMEM((STREAMS, 2 * HIDDEN), f32),
            pltpu.VMEM((CHIPS, STREAMS, WIDE), f32),
            pltpu.VMEM((CHIPS, STREAMS, WIDE), bf16),
            pltpu.VMEM((CHIPS, STREAMS, WIDE), bf16),
            pltpu.VMEM((CHIPS, COLS, SUB, WIDE), bf16),
            pltpu.VMEM((CHIPS, COLS, SUB, WIDE), bf16),
            pltpu.VMEM((SUB, WIDE), bf16),
            dma((7,)),
            dma((TURNS, 4)),
            dma((COLS,)),
            dma((COLS,)),
            dma((ROWS,)),
            dma((ROWS,)),
            dma((COLS,)),
            dma((TURNS, COLS)),
            dma((ROWS,)),
            dma((ROWS,)),
            dma((ROWS,)),
            dma((ROWS,)),
            dma((COLS,)),
            dma((COLS,)),
            dma((PEERS,)),
            dma((CHIPS, COLS)),
            dma((CHIPS,)),
            dma((CHIPS,)),
            dma((CHIPS,)),
            dma((CHIPS,)),
            dma((CHIPS, COLS)),
            dma((CHIPS, COLS)),
        ],
        compiler_params=pltpu.CompilerParams(
            collective_id=0, has_side_effects=True, vmem_limit_bytes=56 * 1024 * 1024
        ),
        cost_estimate=pl.CostEstimate(
            flops=TURNS * 2 * STREAMS * 9830400, bytes_accessed=24_000_000, transcendentals=0
        ),
    )(
        lengths,
        hidden,
        attn_gain,
        ffn_gain,
        q_weight,
        key_weight,
        value_weight,
        out_weight,
        gate_weight,
        up_weight,
        down_weight,
        key_cache,
        value_cache,
    )


def solution(mesh):
    return jax.shard_map(
        per_device,
        mesh=mesh,
        in_specs=(
            P("section", None, ("row", "col")),
            P(None, "row"),
            P("section", ("row", "col")),
            P("section", ("row", "col")),
            P("section", "row", "col"),
            P("section", "row", "col"),
            P("section", "row", "col"),
            P("section", "col", "row"),
            P("section", None, ("row", "col")),
            P("section", None, ("row", "col")),
            P("section", ("row", "col"), None),
            P("section", None, "row", "col", None, None),
            P("section", None, "row", "col", None, None),
        ),
        out_specs=P("section", None, ("row", "col")),
        check_vma=False,
    )
```

```python
import functools
import math

import jax
import jax.numpy as jnp
from jax import lax
from jax.experimental import pallas as pl
from jax.experimental.pallas import tpu as pltpu
from jax.sharding import PartitionSpec as P

D = 5120
HD = 128
CTX = 96
TURNS = 4
ROWS = 8
COLS = 4
CHIPS = 4
PEERS = 16
WIDE = 640
PIECE = 160
SUB = 16
STREAMS = 64
LOCAL = 8
KVSPLIT = 2
QKV = 896
PACK = 512
OPACK = 384
HIDDEN = 512
norm_eps = 1e-06
masked_score = -1e30
f32 = jnp.float32
bf16 = jnp.bfloat16


def remote(src, dst, send, recv, device):
    return pltpu.make_async_remote_copy(
        src_ref=src,
        dst_ref=dst,
        send_sem=send,
        recv_sem=recv,
        device_id=device,
        device_id_type=pl.DeviceIdType.MESH,
    )


def kernel(
    len_hbm,
    hid_hbm,
    ag_hbm,
    fg_hbm,
    wq_hbm,
    wk_hbm,
    wv_hbm,
    wo_hbm,
    wg_hbm,
    wu_hbm,
    wd_hbm,
    kc_hbm,
    vc_hbm,
    out_ref,
    len_ref,
    hid_ref,
    ag_ref,
    fg_ref,
    wqkv,
    wo,
    wgu,
    wd,
    kc,
    vc,
    init,
    gain1,
    gain2,
    bias,
    xin,
    s2,
    r2,
    o3,
    s4,
    r4,
    x2_all,
    acc,
    keep,
    p6,
    q6,
    s6,
    r6,
    x_send,
    isem,
    wsem,
    csem,
    zready,
    send0,
    recv0,
    sendg,
    recvg,
    send1,
    recv1,
    send2,
    recv2,
    send3,
    recv3,
    send4,
    recv4,
    send5,
    recv5,
    send_f,
    recv_f,
    send_p,
    recv_p,
    send6,
    recv6,
):
    s = lax.axis_index("section")
    r = lax.axis_index("row")
    c = lax.axis_index("col")
    x_chip = r // 2
    core = lax.rem(r, 2)
    pair = 2 * x_chip + 1 - core
    s_next = lax.rem(s + 1, TURNS)
    s_prev = lax.rem(s + TURNS - 1, TURNS)

    def row_at(i):
        return lax.rem(r + i, ROWS)

    def col_at(i):
        return lax.rem(c + i, COLS)

    inputs = [
        pltpu.make_async_copy(hid_hbm, hid_ref, isem.at[0]),
        pltpu.make_async_copy(ag_hbm, ag_ref, isem.at[1]),
        pltpu.make_async_copy(fg_hbm, fg_ref, isem.at[2]),
        pltpu.make_async_copy(len_hbm, len_ref, isem.at[3]),
    ]
    weight_copies = []
    for g in range(KVSPLIT):
        for source, first, width in ((wq_hbm, 0, WIDE), (wk_hbm, WIDE, HD), (wv_hbm, WIDE + HD, HD)):
            weight_copies.append(
                pltpu.make_async_copy(
                    source.at[0, :, pl.ds(g * width, width)],
                    wqkv.at[:, pl.ds(g * QKV + first, width)],
                    wsem.at[len(weight_copies)],
                )
            )
    weight_copies += [
        pltpu.make_async_copy(wo_hbm.at[0], wo, wsem.at[6]),
        pltpu.make_async_copy(wg_hbm.at[0], wgu.at[:, pl.ds(0, HIDDEN)], wsem.at[7]),
        pltpu.make_async_copy(wu_hbm.at[0], wgu.at[:, pl.ds(HIDDEN, HIDDEN)], wsem.at[8]),
        pltpu.make_async_copy(wd_hbm.at[0], wd, wsem.at[9]),
    ]

    def cache_copies(t):
        m = lax.rem(s + TURNS - t, TURNS)
        copies = []
        for g in range(2):
            copies.append(
                pltpu.make_async_copy(kc_hbm.at[0, m, :, g], kc.at[t, g], csem.at[t, g])
            )
            copies.append(
                pltpu.make_async_copy(vc_hbm.at[0, m, :, g], vc.at[t, g], csem.at[t, 2 + g])
            )
        return copies

    barrier = pltpu.get_barrier_semaphore()
    greeted = [(s, row_at(i), c) for i in range(1, ROWS)]
    greeted += [(s, r, col_at(i)) for i in range(1, COLS)]
    greeted += [(s_prev, r, c), (s_next, r, c)]
    for device in greeted:
        pl.semaphore_signal(
            barrier, inc=1, device_id=device, device_id_type=pl.DeviceIdType.MESH
        )

    def row_of(dx):
        return 2 * lax.rem(x_chip + dx, CHIPS) + core

    for copy in inputs + weight_copies[:6]:
        copy.start()
    for copy in cache_copies(0):
        copy.start()
    for copy in weight_copies[6:]:
        copy.start()
    for t in range(1, TURNS):
        for copy in cache_copies(t):
            copy.start()
    for copy in inputs:
        copy.wait()

    init[c] = jnp.zeros((80, 256), bf16)
    init[c, 0:64, 0:PIECE] = hid_ref[0]
    gain_row = lax.broadcasted_iota(jnp.int32, (SUB, PIECE), 0)
    init[c, 64:80, 0:PIECE] = jnp.where(
        gain_row == 0, ag_ref[...].astype(f32), fg_ref[...].astype(f32)
    ).astype(bf16)

    pl.semaphore_wait(barrier, len(greeted))

    def send_init(i):
        return remote(
            init.at[c], init.at[c], send0.at[i], recv0.at[c], (s, r, col_at(i))
        )

    def wait_init(i):
        return remote(
            init.at[col_at(i)], init.at[col_at(i)], send0.at[i], recv0.at[col_at(i)],
            (s, r, col_at(i)),
        )

    for i in (2, 1, 3):
        send_init(i).start()
    stream_row = lax.broadcasted_iota(jnp.int32, (LOCAL, LOCAL * CTX), 0)
    position = lax.broadcasted_iota(jnp.int32, (LOCAL, LOCAL * CTX), 1)
    for t in range(TURNS):
        m = lax.rem(s + TURNS - t, TURNS)
        offsets = jnp.full((LOCAL, LOCAL * CTX), masked_score, f32)
        for b in range(LOCAL):
            live = (
                (stream_row == b)
                & (position >= b * CTX)
                & (position < b * CTX + len_ref[m, b])
            )
            offsets = jnp.where(live, 0.0, offsets)
        bias[t] = offsets

    for i in range(1, COLS):
        wait_init(i).wait_recv()
    pl.semaphore_signal(
        zready, inc=1, device_id=(s_prev, r, c), device_id_type=pl.DeviceIdType.MESH
    )
    joined = None
    for i in range(COLS):
        piece = jnp.concatenate(
            [init[i].astype(f32), jnp.zeros((80, WIDE - 256), f32)], axis=1
        )
        if i:
            piece = pltpu.roll(piece, i * PIECE, 1)
        joined = piece if joined is None else joined + piece
    xin[0] = joined[0:64].astype(bf16).reshape(COLS, SUB, WIDE)
    gain1[...] = joined[64:65]
    gain2[r] = jnp.broadcast_to(joined[65:66], (8, WIDE))

    def send_gain(i):
        return remote(
            gain2.at[r], gain2.at[r], sendg.at[i], recvg.at[r], (s, row_at(i), c)
        )

    def wait_gain(i):
        return remote(
            gain2.at[row_at(i)], gain2.at[row_at(i)], sendg.at[i], recvg.at[row_at(i)],
            (s, row_at(i), c),
        )

    def turn(t, _):
        x_all = xin[t].reshape(STREAMS, WIDE).astype(f32)
        squares = jnp.sum(x_all * x_all, axis=1, keepdims=True)
        high = squares.astype(bf16).astype(f32)
        low = squares - high
        left = (x_all * gain1[...]).astype(bf16)

        @pl.when(t == 0)
        def _():
            for copy in weight_copies[:6]:
                copy.wait()

        lane = lax.broadcasted_iota(jnp.int32, (STREAMS, 128), 1)
        sums = jnp.where(lane < 64, high, low).reshape(ROWS, LOCAL, 128)

        def send_two(g, i):
            return remote(
                s2.at[g, row_at(i)], r2.at[g, r], send2.at[g, i], recv2.at[g, r],
                (s, row_at(i), c),
            )

        def wait_two(g, i):
            return remote(
                s2.at[g, row_at(i)], r2.at[g, row_at(i)], send2.at[g, i],
                recv2.at[g, row_at(i)], (s, row_at(i), c),
            )

        for g in range(KVSPLIT):
            part = jnp.dot(
                left, wqkv[:, g * QKV:(g + 1) * QKV], preferred_element_type=f32
            ).reshape(ROWS, LOCAL, QKV)
            rest = jnp.concatenate([part[:, :, PACK:QKV], sums], axis=2)
            s2[g] = jnp.concatenate([part[:, :, 0:PACK], rest], axis=1).astype(bf16)
            for i in (4, 3, 5, 2, 6, 1, 7):
                send_two(g, i).start()

        @pl.when(t == 0)
        def _():
            for i in range(1, ROWS):
                send_gain(i).start()

        @pl.when(t == 0)
        def _():
            for copy in cache_copies(0):
                copy.wait()

        @pl.when(t > 0)
        def _():
            for copy in cache_copies(t):
                copy.wait()

        def send_three(g, i):
            return remote(
                o3.at[g, r], o3.at[g, r], send3.at[g, i], recv3.at[g, r], (s, row_at(i), c)
            )

        def wait_three(g, i):
            return remote(
                o3.at[g, row_at(i)], o3.at[g, row_at(i)], send3.at[g, i],
                recv3.at[g, row_at(i)], (s, row_at(i), c),
            )

        score_scale = 1.0 / math.sqrt(HD)
        offsets = jnp.concatenate([bias[t]] * 5, axis=0)
        for g in range(KVSPLIT):
            total = s2[g, r].astype(f32)
            for i in (1, 7, 2, 6, 3, 5, 4):
                wait_two(g, i).wait_recv()
                total = total + r2[g, row_at(i)].astype(f32)
            top, bottom = total[0:8], total[8:16]
            mean_square = (bottom[:, 384:385] + bottom[:, 448:449]) / D
            scale = lax.rsqrt(mean_square + norm_eps)
            top = (top * scale).astype(bf16).astype(f32)
            bottom = (bottom[:, 0:384] * scale).astype(bf16).astype(f32)
            queries = jnp.concatenate(
                [top[:, j * HD:(j + 1) * HD] for j in range(4)] + [bottom[:, 0:HD]], axis=0
            )
            key_new = jnp.concatenate([bottom[:, HD:2 * HD]] * 5, axis=0)
            value_new = jnp.concatenate([bottom[:, 2 * HD:3 * HD]] * 5, axis=0)
            keys = kc[t, g].reshape(LOCAL * CTX, HD)
            values = vc[t, g].reshape(LOCAL * CTX, HD)
            scores = lax.dot_general(
                queries.astype(bf16), keys, (((1,), (1,)), ((), ())),
                preferred_element_type=f32,
            )
            scores = scores * score_scale + offsets
            self_score = jnp.sum(queries * key_new, axis=1, keepdims=True) * score_scale
            row_max = jnp.maximum(jnp.max(scores, axis=1, keepdims=True), self_score)
            weights = jnp.exp(scores - row_max)
            self_weight = jnp.exp(self_score - row_max)
            denominator = jnp.sum(weights, axis=1, keepdims=True) + self_weight
            probs = (weights / denominator).astype(bf16)
            self_prob = (self_weight / denominator).astype(bf16).astype(f32)
            mixed = jnp.dot(probs, values, preferred_element_type=f32)
            mixed = mixed + self_prob * value_new
            heads = [mixed[j * 8:(j + 1) * 8] for j in range(5)]
            o3[g, r] = jnp.concatenate(
                [
                    jnp.concatenate(heads[0:3], axis=1),
                    jnp.concatenate(heads[3:5] + [jnp.zeros((LOCAL, HD), f32)], axis=1),
                ],
                axis=0,
            ).astype(bf16)
            for i in (4, 3, 5, 2, 6, 1, 7):
                send_three(g, i).start()

        @pl.when(t == 0)
        def _():
            weight_copies[6].wait()

        out_part = None
        for g in range(KVSPLIT):
            for i in (1, 7, 2, 6, 3, 5, 4):
                wait_three(g, i).wait_recv()
            gathered = o3[g].astype(f32)
            heads = jnp.concatenate(
                [
                    gathered[:, 0:8].reshape(STREAMS, OPACK),
                    gathered[:, 8:16, 0:WIDE - OPACK].reshape(STREAMS, WIDE - OPACK),
                ],
                axis=1,
            ).astype(bf16)
            product = jnp.dot(
                heads, wo[g * WIDE:(g + 1) * WIDE, :], preferred_element_type=f32
            )
            out_part = product if out_part is None else out_part + product
        s4[...] = out_part.astype(bf16).reshape(COLS, SUB, WIDE)

        def send_four(i):
            return remote(
                s4.at[col_at(i)], r4.at[c], send4.at[i], recv4.at[c], (s, r, col_at(i))
            )

        def wait_four(i):
            return remote(
                s4.at[col_at(i)], r4.at[col_at(i)], send4.at[i], recv4.at[col_at(i)],
                (s, r, col_at(i)),
            )

        for i in (2, 1, 3):
            send_four(i).start()
        after = xin[t, c].astype(f32) + s4[c].astype(f32)
        for i in (1, 3, 2):
            wait_four(i).wait_recv()
            after = after + r4[col_at(i)].astype(f32)
        x2_all[r, c] = after.astype(bf16)
        after = x2_all[r, c].astype(f32)

        def send_five(i):
            return remote(
                x2_all.at[r, c], x2_all.at[r, c], send5.at[i], recv5.at[x_chip, c],
                (s, row_of(i // COLS), col_at(i % COLS)),
            )

        for i in (2, 1, 3, 6, 14, 5, 7, 13, 15, 4, 12, 10, 9, 11, 8):
            send_five(i).start()

        @pl.when(t == 0)
        def _():
            for i in range(1, ROWS):
                wait_gain(i).wait_recv()
            for copy in weight_copies[7:9]:
                copy.wait()

        acc[...] = jnp.zeros_like(acc)

        def chip_at(j):
            return lax.rem(x_chip + j + (j // 2) * (5 - 2 * j), 4)

        def forward(xc):
            row = 2 * xc + core
            return remote(
                x2_all.at[row], x2_all.at[row], send_f.at[xc], recv_f.at[xc], (s, pair, c)
            )

        def collect(j):
            xc = chip_at(j)
            for q in range(COLS):

                @pl.when((xc != x_chip) | (q != c))
                def _():
                    row = 2 * xc + core
                    remote(
                        x2_all.at[row, q], x2_all.at[row, q], send5.at[0],
                        recv5.at[xc, q], (s, pair, c),
                    ).wait_recv()

            forward(xc).start()

        def gate_step(j, squares):
            @pl.when(j < CHIPS - 1)
            def _():
                collect(j + 1)

            xc = chip_at(j)
            row = 2 * xc + 1 - core
            remote(
                x2_all.at[row], x2_all.at[row], send_f.at[xc], recv_f.at[xc], (s, pair, c)
            ).wait_recv()
            values = jnp.concatenate(
                [x2_all[2 * xc + k].reshape(STREAMS, WIDE) for k in range(2)], axis=1
            ).astype(f32)
            gains = jnp.concatenate([gain2[2 * xc + k, 0:1] for k in range(2)], axis=1)
            square = values * values
            for k in range(10):
                squares = squares + square[:, k * 128:(k + 1) * 128]
            scaled = (values * gains).astype(bf16)
            first = pl.multiple_of(xc * 1280, 1280)
            acc[...] += jnp.dot(
                scaled, wgu[pl.ds(first, 1280), :], preferred_element_type=f32
            )
            return squares

        collect(0)
        squares = lax.fori_loop(0, CHIPS, gate_step, jnp.zeros((STREAMS, 128), f32))
        mean_square = jnp.sum(squares, axis=1, keepdims=True) / D
        scale = lax.rsqrt(mean_square + norm_eps)
        gate = acc[:, 0:HIDDEN] * scale
        up = acc[:, HIDDEN:2 * HIDDEN] * scale
        activation = (gate / (1.0 + jnp.exp(-gate)) * up).astype(bf16)

        @pl.when(t == 0)
        def _():
            weight_copies[9].wait()

        def swap(xc):
            return remote(
                p6.at[xc], q6.at[xc], send_p.at[xc], recv_p.at[xc], (s, pair, c)
            )

        def down_step(j, _):
            xc = chip_at(CHIPS - 1 - j)
            first = pl.multiple_of(xc * 1280, 1280)
            part = jnp.dot(
                activation, wd[:, pl.ds(first, 1280)], preferred_element_type=f32
            )
            lower, upper = part[:, 0:WIDE], part[:, WIDE:1280]
            keep[xc] = jnp.where(core == 0, lower, upper)
            p6[xc] = jnp.where(core == 0, upper, lower).astype(bf16)
            swap(xc).start()
            return 0

        lax.fori_loop(0, CHIPS, down_step, 0)

        def send_six(xc, i):
            q = col_at(i)
            return remote(
                s6.at[xc, q], r6.at[x_chip, c], send6.at[xc, i], recv6.at[x_chip, c],
                (s, 2 * xc + core, q),
            )

        def share_step(j, _):
            xc = chip_at(CHIPS - 1 - j)
            swap(xc).wait_recv()
            both = keep[xc] + q6[xc].astype(f32)
            s6[xc] = both.astype(bf16).reshape(COLS, SUB, WIDE)
            for i in (2, 1, 3):
                send_six(xc, i).start()

            @pl.when(xc != x_chip)
            def _():
                send_six(xc, 0).start()

            return 0

        lax.fori_loop(0, CHIPS, share_step, 0)

        def sum_step(j, total):
            xc = chip_at(j)
            for i in (1, 3, 2):
                q = col_at(i)
                remote(
                    s6.at[xc, q], r6.at[xc, q], send6.at[xc, i], recv6.at[xc, q],
                    (s, pair, c),
                ).wait_recv()
                total = total + r6[xc, q].astype(f32)
            return total

        total = sum_step(0, after + s6[x_chip, c].astype(f32))

        def far_step(j, total):
            xc = chip_at(j)
            remote(
                s6.at[xc, c], r6.at[xc, c], send6.at[xc, 0], recv6.at[xc, c], (s, pair, c)
            ).wait_recv()
            return sum_step(j, total + r6[xc, c].astype(f32))

        total = lax.fori_loop(1, CHIPS, far_step, total)
        x_send[...] = total.astype(bf16)

        def send_one(i):
            return remote(
                x_send, xin.at[t + 1, c], send1.at[i], recv1.at[t, c],
                (s_next, r, col_at(i)),
            )

        def wait_one(i):
            return remote(
                x_send, xin.at[t + 1, col_at(i)], send1.at[i], recv1.at[t, col_at(i)],
                (s_next, r, col_at(i)),
            )

        @pl.when(t == 0)
        def _():
            pl.semaphore_wait(zready, 1)

        for i in (2, 1, 3, 0):
            send_one(i).start()

        for g in range(KVSPLIT):
            for i in range(1, ROWS):
                send_two(g, i).wait_send()
                send_three(g, i).wait_send()
        for i in range(1, COLS):
            send_four(i).wait_send()

        for i in range(1, PEERS):
            send_five(i).wait_send()
        for i in range(CHIPS):
            forward(i).wait_send()
            swap(i).wait_send()
            for k in range(1, COLS):
                send_six(i, k).wait_send()

            @pl.when(i != x_chip)
            def _():
                send_six(i, 0).wait_send()

        for i in range(COLS):
            send_one(i).wait_send()
        for i in range(COLS):
            wait_one(i).wait_recv()
        return 0

    lax.fori_loop(0, TURNS, turn, 0)

    final = xin[TURNS].reshape(STREAMS, WIDE).astype(f32)
    final = pltpu.roll(final, lax.rem(WIDE - c * PIECE, WIDE), 1)
    out_ref[0] = final[:, 0:PIECE].astype(bf16)
    for i in range(1, COLS):
        send_init(i).wait_send()
    for i in range(1, ROWS):
        send_gain(i).wait_send()


def per_device(
    hidden,
    lengths,
    attn_gain,
    ffn_gain,
    q_weight,
    key_weight,
    value_weight,
    out_weight,
    gate_weight,
    up_weight,
    down_weight,
    key_cache,
    value_cache,
):
    vmem = pl.BlockSpec(memory_space=pltpu.VMEM)
    hbm = pl.BlockSpec(memory_space=pl.ANY)
    dma = pltpu.SemaphoreType.DMA
    return pl.pallas_call(
        kernel,
        out_shape=jax.ShapeDtypeStruct((1, STREAMS, PIECE), bf16),
        in_specs=[hbm] * 13,
        out_specs=vmem,
        scratch_shapes=[
            pltpu.SMEM((TURNS, LOCAL), jnp.int32),
            pltpu.VMEM((1, STREAMS, PIECE), bf16),
            pltpu.VMEM((1, PIECE), bf16),
            pltpu.VMEM((1, PIECE), bf16),
            pltpu.VMEM((WIDE, KVSPLIT * QKV), bf16),
            pltpu.VMEM((1280, WIDE), bf16),
            pltpu.VMEM((D, 2 * HIDDEN), bf16),
            pltpu.VMEM((HIDDEN, D), bf16),
            pltpu.VMEM((TURNS, 2, LOCAL, CTX, HD), bf16),
            pltpu.VMEM((TURNS, 2, LOCAL, CTX, HD), bf16),
            pltpu.VMEM((COLS, 80, 256), bf16),
            pltpu.VMEM((1, WIDE), f32),
            pltpu.VMEM((ROWS, 8, WIDE), f32),
            pltpu.VMEM((TURNS, LOCAL, LOCAL * CTX), f32),
            pltpu.VMEM((TURNS + 1, COLS, SUB, WIDE), bf16),
            pltpu.VMEM((KVSPLIT, ROWS, SUB, PACK), bf16),
            pltpu.VMEM((KVSPLIT, ROWS, SUB, PACK), bf16),
            pltpu.VMEM((KVSPLIT, ROWS, SUB, OPACK), bf16),
            pltpu.VMEM((COLS, SUB, WIDE), bf16),
            pltpu.VMEM((COLS, SUB, WIDE), bf16),
            pltpu.VMEM((ROWS, COLS, SUB, WIDE), bf16),
            pltpu.VMEM((STREAMS, 2 * HIDDEN), f32),
            pltpu.VMEM((CHIPS, STREAMS, WIDE), f32),
            pltpu.VMEM((CHIPS, STREAMS, WIDE), bf16),
            pltpu.VMEM((CHIPS, STREAMS, WIDE), bf16),
            pltpu.VMEM((CHIPS, COLS, SUB, WIDE), bf16),
            pltpu.VMEM((CHIPS, COLS, SUB, WIDE), bf16),
            pltpu.VMEM((SUB, WIDE), bf16),
            dma((4,)),
            dma((10,)),
            dma((TURNS, 4)),
            pltpu.SemaphoreType.REGULAR,
            dma((COLS,)),
            dma((COLS,)),
            dma((ROWS,)),
            dma((ROWS,)),
            dma((COLS,)),
            dma((TURNS, COLS)),
            dma((KVSPLIT, ROWS)),
            dma((KVSPLIT, ROWS)),
            dma((KVSPLIT, ROWS)),
            dma((KVSPLIT, ROWS)),
            dma((COLS,)),
            dma((COLS,)),
            dma((PEERS,)),
            dma((CHIPS, COLS)),
            dma((CHIPS,)),
            dma((CHIPS,)),
            dma((CHIPS,)),
            dma((CHIPS,)),
            dma((CHIPS, COLS)),
            dma((CHIPS, COLS)),
        ],
        compiler_params=pltpu.CompilerParams(
            collective_id=0, has_side_effects=True, vmem_limit_bytes=56 * 1024 * 1024
        ),
        cost_estimate=pl.CostEstimate(
            flops=TURNS * 2 * STREAMS * 9830400, bytes_accessed=24_000_000, transcendentals=0
        ),
    )(
        lengths,
        hidden,
        attn_gain,
        ffn_gain,
        q_weight,
        key_weight,
        value_weight,
        out_weight,
        gate_weight,
        up_weight,
        down_weight,
        key_cache,
        value_cache,
    )


def solution(mesh):
    return jax.shard_map(
        per_device,
        mesh=mesh,
        in_specs=(
            P("section", None, ("row", "col")),
            P(None, "row"),
            P("section", ("row", "col")),
            P("section", ("row", "col")),
            P("section", "row", "col"),
            P("section", "row", "col"),
            P("section", "row", "col"),
            P("section", "col", "row"),
            P("section", None, ("row", "col")),
            P("section", None, ("row", "col")),
            P("section", ("row", "col"), None),
            P("section", None, "row", "col", None, None),
            P("section", None, "row", "col", None, None),
        ),
        out_specs=P("section", None, ("row", "col")),
        check_vma=False,
    )
```

```python
import functools
import math

import jax
import jax.numpy as jnp
from jax import lax
from jax.experimental import pallas as pl
from jax.experimental.pallas import tpu as pltpu
from jax.sharding import PartitionSpec as P

D = 5120
HD = 128
CTX = 96
TURNS = 4
ROWS = 8
COLS = 4
CHIPS = 4
PEERS = 16
WIDE = 640
PIECE = 160
SUB = 16
STREAMS = 64
LOCAL = 8
KVSPLIT = 2
QKV = 896
PACK = 512
OPACK = 384
HIDDEN = 512
norm_eps = 1e-06
masked_score = -1e30
f32 = jnp.float32
bf16 = jnp.bfloat16


def remote(src, dst, send, recv, device):
    return pltpu.make_async_remote_copy(
        src_ref=src,
        dst_ref=dst,
        send_sem=send,
        recv_sem=recv,
        device_id=device,
        device_id_type=pl.DeviceIdType.MESH,
    )


def kernel(
    len_hbm,
    hid_hbm,
    ag_hbm,
    fg_hbm,
    wq_hbm,
    wk_hbm,
    wv_hbm,
    wo_hbm,
    wg_hbm,
    wu_hbm,
    wd_hbm,
    kc_hbm,
    vc_hbm,
    out_ref,
    len_ref,
    hid_ref,
    ag_ref,
    fg_ref,
    wqkv,
    wo,
    wgu,
    wd,
    kc,
    vc,
    init,
    gain1,
    gain2,
    bias,
    xin,
    s2,
    r2,
    o3,
    s4,
    r4,
    x2_all,
    acc,
    mine,
    theirs,
    s6,
    r6,
    x_send,
    isem,
    wsem,
    csem,
    zready,
    send0,
    recv0,
    sendg,
    recvg,
    send1,
    recv1,
    send2,
    recv2,
    send3,
    recv3,
    send4,
    recv4,
    send5,
    recv5,
    send_p,
    recv_p,
    send_w,
    recv_w,
    send6,
    recv6,
):
    s = lax.axis_index("section")
    r = lax.axis_index("row")
    c = lax.axis_index("col")
    x_chip = r // 2
    core = lax.rem(r, 2)
    pair = 2 * x_chip + 1 - core
    s_next = lax.rem(s + 1, TURNS)
    s_prev = lax.rem(s + TURNS - 1, TURNS)

    def row_at(i):
        return lax.rem(r + i, ROWS)

    def col_at(i):
        return lax.rem(c + i, COLS)

    inputs = [
        pltpu.make_async_copy(hid_hbm, hid_ref, isem.at[0]),
        pltpu.make_async_copy(ag_hbm, ag_ref, isem.at[1]),
        pltpu.make_async_copy(fg_hbm, fg_ref, isem.at[2]),
        pltpu.make_async_copy(len_hbm, len_ref, isem.at[3]),
    ]
    weight_copies = []
    for g in range(KVSPLIT):
        for source, first, width in ((wq_hbm, 0, WIDE), (wk_hbm, WIDE, HD), (wv_hbm, WIDE + HD, HD)):
            weight_copies.append(
                pltpu.make_async_copy(
                    source.at[0, :, pl.ds(g * width, width)],
                    wqkv.at[:, pl.ds(g * QKV + first, width)],
                    wsem.at[len(weight_copies)],
                )
            )
    weight_copies += [
        pltpu.make_async_copy(wo_hbm.at[0], wo, wsem.at[6]),
        pltpu.make_async_copy(
            wg_hbm.at[:, core], wgu.at[core, :, :, pl.ds(0, HIDDEN)], wsem.at[7]
        ),
        pltpu.make_async_copy(
            wu_hbm.at[:, core], wgu.at[core, :, :, pl.ds(HIDDEN, HIDDEN)], wsem.at[8]
        ),
    ]
    other_copies = [
        remote(
            wg_hbm.at[:, 1 - core], wgu.at[core, :, :, pl.ds(0, HIDDEN)],
            send_w.at[0], recv_w.at[0], (s, pair, c),
        ),
        remote(
            wu_hbm.at[:, 1 - core], wgu.at[core, :, :, pl.ds(HIDDEN, HIDDEN)],
            send_w.at[1], recv_w.at[1], (s, pair, c),
        ),
    ]
    for i in range(CHIPS):
        ours = pl.multiple_of((2 * i + core) * WIDE, WIDE)
        other = pl.multiple_of((2 * i + 1 - core) * WIDE, WIDE)
        weight_copies.append(
            pltpu.make_async_copy(
                wd_hbm.at[0, :, pl.ds(ours, WIDE)],
                wd.at[core, :, pl.ds(i * WIDE, WIDE)],
                wsem.at[9 + i],
            )
        )
        other_copies.append(
            remote(
                wd_hbm.at[0, :, pl.ds(other, WIDE)], wd.at[core, :, pl.ds(i * WIDE, WIDE)],
                send_w.at[2 + i], recv_w.at[2 + i], (s, pair, c),
            )
        )

    def wait_other(i):
        if i < 2:
            place = wgu.at[1 - core, :, :, pl.ds(i * HIDDEN, HIDDEN)]
        else:
            place = wd.at[1 - core, :, pl.ds((i - 2) * WIDE, WIDE)]
        remote(place, place, send_w.at[i], recv_w.at[i], (s, pair, c)).wait_recv()

    def cache_copies(t):
        m = lax.rem(s + TURNS - t, TURNS)
        copies = []
        for g in range(2):
            copies.append(
                pltpu.make_async_copy(kc_hbm.at[0, m, :, g], kc.at[t, g], csem.at[t, g])
            )
            copies.append(
                pltpu.make_async_copy(vc_hbm.at[0, m, :, g], vc.at[t, g], csem.at[t, 2 + g])
            )
        return copies

    barrier = pltpu.get_barrier_semaphore()
    greeted = [(s, row_at(i), c) for i in range(1, ROWS)]
    greeted += [(s, r, col_at(i)) for i in range(1, COLS)]
    greeted += [(s_prev, r, c), (s_next, r, c)]
    for device in greeted:
        pl.semaphore_signal(
            barrier, inc=1, device_id=device, device_id_type=pl.DeviceIdType.MESH
        )

    def row_of(dx):
        return 2 * lax.rem(x_chip + dx, CHIPS) + core

    for copy in inputs + weight_copies[:6]:
        copy.start()
    for copy in cache_copies(0):
        copy.start()
    for copy in weight_copies[6:]:
        copy.start()
    for t in range(1, TURNS):
        for copy in cache_copies(t):
            copy.start()
    for copy in inputs:
        copy.wait()

    init[c] = jnp.zeros((80, 256), bf16)
    init[c, 0:64, 0:PIECE] = hid_ref[0]
    gain_row = lax.broadcasted_iota(jnp.int32, (SUB, PIECE), 0)
    init[c, 64:80, 0:PIECE] = jnp.where(
        gain_row == 0, ag_ref[...].astype(f32), fg_ref[...].astype(f32)
    ).astype(bf16)

    pl.semaphore_wait(barrier, len(greeted))

    def send_init(i):
        return remote(
            init.at[c], init.at[c], send0.at[i], recv0.at[c], (s, r, col_at(i))
        )

    def wait_init(i):
        return remote(
            init.at[col_at(i)], init.at[col_at(i)], send0.at[i], recv0.at[col_at(i)],
            (s, r, col_at(i)),
        )

    for i in (2, 1, 3):
        send_init(i).start()
    for copy in other_copies[:1]:
        copy.start()
    stream_row = lax.broadcasted_iota(jnp.int32, (LOCAL, LOCAL * CTX), 0)
    position = lax.broadcasted_iota(jnp.int32, (LOCAL, LOCAL * CTX), 1)
    for t in range(TURNS):
        m = lax.rem(s + TURNS - t, TURNS)
        offsets = jnp.full((LOCAL, LOCAL * CTX), masked_score, f32)
        for b in range(LOCAL):
            live = (
                (stream_row == b)
                & (position >= b * CTX)
                & (position < b * CTX + len_ref[m, b])
            )
            offsets = jnp.where(live, 0.0, offsets)
        bias[t] = offsets

    for i in range(1, COLS):
        wait_init(i).wait_recv()
    pl.semaphore_signal(
        zready, inc=1, device_id=(s_prev, r, c), device_id_type=pl.DeviceIdType.MESH
    )
    joined = None
    for i in range(COLS):
        piece = jnp.concatenate(
            [init[i].astype(f32), jnp.zeros((80, WIDE - 256), f32)], axis=1
        )
        if i:
            piece = pltpu.roll(piece, i * PIECE, 1)
        joined = piece if joined is None else joined + piece
    xin[0] = joined[0:64].astype(bf16).reshape(COLS, SUB, WIDE)
    gain1[...] = joined[64:65]
    gain2[r] = jnp.broadcast_to(joined[65:66], (8, WIDE))

    def send_gain(i):
        return remote(
            gain2.at[r], gain2.at[r], sendg.at[i], recvg.at[r], (s, row_at(i), c)
        )

    def wait_gain(i):
        return remote(
            gain2.at[row_at(i)], gain2.at[row_at(i)], sendg.at[i], recvg.at[row_at(i)],
            (s, row_at(i), c),
        )

    def turn(t, _):
        x_all = xin[t].reshape(STREAMS, WIDE).astype(f32)
        squares = jnp.sum(x_all * x_all, axis=1, keepdims=True)
        high = squares.astype(bf16).astype(f32)
        low = squares - high
        left = (x_all * gain1[...]).astype(bf16)

        @pl.when(t == 0)
        def _():
            for copy in weight_copies[:6]:
                copy.wait()

        lane = lax.broadcasted_iota(jnp.int32, (STREAMS, 128), 1)
        sums = jnp.where(lane < 64, high, low).reshape(ROWS, LOCAL, 128)

        def send_two(g, i):
            return remote(
                s2.at[g, row_at(i)], r2.at[g, r], send2.at[g, i], recv2.at[g, r],
                (s, row_at(i), c),
            )

        def wait_two(g, i):
            return remote(
                s2.at[g, row_at(i)], r2.at[g, row_at(i)], send2.at[g, i],
                recv2.at[g, row_at(i)], (s, row_at(i), c),
            )

        for g in range(KVSPLIT):
            part = jnp.dot(
                left, wqkv[:, g * QKV:(g + 1) * QKV], preferred_element_type=f32
            ).reshape(ROWS, LOCAL, QKV)
            rest = jnp.concatenate([part[:, :, PACK:QKV], sums], axis=2)
            s2[g] = jnp.concatenate([part[:, :, 0:PACK], rest], axis=1).astype(bf16)
            for i in (4, 3, 5, 2, 6, 1, 7):
                send_two(g, i).start()

        @pl.when(t == 0)
        def _():
            for i in (2, 4, 6):
                send_gain(i).start()
            other_copies[1].start()

        @pl.when(t == 0)
        def _():
            for copy in cache_copies(0):
                copy.wait()

        @pl.when(t > 0)
        def _():
            for copy in cache_copies(t):
                copy.wait()

        def send_three(g, i):
            return remote(
                o3.at[g, r], o3.at[g, r], send3.at[g, i], recv3.at[g, r], (s, row_at(i), c)
            )

        def wait_three(g, i):
            return remote(
                o3.at[g, row_at(i)], o3.at[g, row_at(i)], send3.at[g, i],
                recv3.at[g, row_at(i)], (s, row_at(i), c),
            )

        score_scale = 1.0 / math.sqrt(HD)
        offsets = jnp.concatenate([bias[t]] * 5, axis=0)
        for g in range(KVSPLIT):
            total = s2[g, r].astype(f32)
            for i in (1, 7, 2, 6, 3, 5, 4):
                wait_two(g, i).wait_recv()
                total = total + r2[g, row_at(i)].astype(f32)
            top, bottom = total[0:8], total[8:16]
            mean_square = (bottom[:, 384:385] + bottom[:, 448:449]) / D
            scale = lax.rsqrt(mean_square + norm_eps)
            top = (top * scale).astype(bf16).astype(f32)
            bottom = (bottom[:, 0:384] * scale).astype(bf16).astype(f32)
            queries = jnp.concatenate(
                [top[:, j * HD:(j + 1) * HD] for j in range(4)] + [bottom[:, 0:HD]], axis=0
            )
            key_new = jnp.concatenate([bottom[:, HD:2 * HD]] * 5, axis=0)
            value_new = jnp.concatenate([bottom[:, 2 * HD:3 * HD]] * 5, axis=0)
            keys = kc[t, g].reshape(LOCAL * CTX, HD)
            values = vc[t, g].reshape(LOCAL * CTX, HD)
            scores = lax.dot_general(
                queries.astype(bf16), keys, (((1,), (1,)), ((), ())),
                preferred_element_type=f32,
            )
            scores = scores * score_scale + offsets
            self_score = jnp.sum(queries * key_new, axis=1, keepdims=True) * score_scale
            row_max = jnp.maximum(jnp.max(scores, axis=1, keepdims=True), self_score)
            weights = jnp.exp(scores - row_max)
            self_weight = jnp.exp(self_score - row_max)
            denominator = jnp.sum(weights, axis=1, keepdims=True) + self_weight
            probs = (weights / denominator).astype(bf16)
            self_prob = (self_weight / denominator).astype(bf16).astype(f32)
            mixed = jnp.dot(probs, values, preferred_element_type=f32)
            mixed = mixed + self_prob * value_new
            heads = [mixed[j * 8:(j + 1) * 8] for j in range(5)]
            o3[g, r] = jnp.concatenate(
                [
                    jnp.concatenate(heads[0:3], axis=1),
                    jnp.concatenate(heads[3:5] + [jnp.zeros((LOCAL, HD), f32)], axis=1),
                ],
                axis=0,
            ).astype(bf16)
            for i in (4, 3, 5, 2, 6, 1, 7):
                send_three(g, i).start()

        @pl.when(t == 0)
        def _():
            weight_copies[6].wait()
            for copy in other_copies[2:]:
                copy.start()

        out_part = None
        for g in range(KVSPLIT):
            for i in (1, 7, 2, 6, 3, 5, 4):
                wait_three(g, i).wait_recv()
            gathered = o3[g].astype(f32)
            heads = jnp.concatenate(
                [
                    gathered[:, 0:8].reshape(STREAMS, OPACK),
                    gathered[:, 8:16, 0:WIDE - OPACK].reshape(STREAMS, WIDE - OPACK),
                ],
                axis=1,
            ).astype(bf16)
            product = jnp.dot(
                heads, wo[g * WIDE:(g + 1) * WIDE, :], preferred_element_type=f32
            )
            out_part = product if out_part is None else out_part + product
        s4[...] = out_part.astype(bf16).reshape(COLS, SUB, WIDE)

        def send_four(i):
            return remote(
                s4.at[col_at(i)], r4.at[c], send4.at[i], recv4.at[c], (s, r, col_at(i))
            )

        def wait_four(i):
            return remote(
                s4.at[col_at(i)], r4.at[col_at(i)], send4.at[i], recv4.at[col_at(i)],
                (s, r, col_at(i)),
            )

        for i in (2, 1, 3):
            send_four(i).start()
        after = xin[t, c].astype(f32) + s4[c].astype(f32)
        for i in (1, 3, 2):
            wait_four(i).wait_recv()
            after = after + r4[col_at(i)].astype(f32)
        x2_all[x_chip, c] = after.astype(bf16)
        after = x2_all[x_chip, c].astype(f32)

        def send_five(i):
            return remote(
                x2_all.at[x_chip, c], x2_all.at[x_chip, c], send5.at[i], recv5.at[x_chip, c],
                (s, row_of(i // COLS), col_at(i % COLS)),
            )

        for i in (2, 1, 3, 6, 14, 5, 7, 13, 15, 4, 12, 10, 9, 11, 8):
            send_five(i).start()

        @pl.when(t == 0)
        def _():
            for i in (2, 4, 6):
                wait_gain(i).wait_recv()
            for copy in weight_copies[7:9]:
                copy.wait()
            for i in range(2):
                wait_other(i)

        def chip_at(j):
            return lax.rem(x_chip + j + (j // 2) * (5 - 2 * j), 4)

        def collect(xc, own):
            for i in (1, 3, 2) if own else (1, 3, 2, 0):
                q = col_at(i)
                remote(
                    x2_all.at[xc, q], x2_all.at[xc, q], send5.at[1], recv5.at[xc, q],
                    (s, pair, c),
                ).wait_recv()
            values = x2_all[xc].reshape(STREAMS, WIDE).astype(f32)
            square = values * values
            squares = square[:, 0:128]
            for k in range(1, 5):
                squares = squares + square[:, k * 128:(k + 1) * 128]
            return (values * gain2[2 * xc + core, 0:1]).astype(bf16), squares

        def gate_part(scaled, xc, h):
            return jnp.dot(scaled, wgu[h, xc], preferred_element_type=f32)

        scaled, squares = collect(x_chip, True)
        for h in range(2):
            acc[h] = gate_part(scaled, x_chip, h)

        def gate_step(j, squares):
            xc = chip_at(j)
            scaled, more = collect(xc, False)
            for h in range(2):
                acc[h] += gate_part(scaled, xc, h)
            return squares + more

        squares = lax.fori_loop(1, CHIPS - 1, gate_step, squares)

        def swap(h):
            return remote(
                mine.at[h], theirs.at[h], send_p.at[h], recv_p.at[h], (s, pair, c)
            )

        far = chip_at(CHIPS - 1)
        scaled, more = collect(far, False)
        squares = jnp.sum(squares + more, axis=1, keepdims=True)
        high = squares.astype(bf16).astype(f32)
        sums = jnp.where(lane < 64, high, squares - high)
        for h in range(2):
            product = acc[h] + gate_part(scaled, far, h)
            acc[h] = product
            mine[h] = jnp.concatenate([product, sums], axis=1).astype(bf16)
            swap(h).start()
        activations = []
        for h in range(2):
            swap(h).wait_recv()
            other = theirs[h].astype(f32)
            if h == 0:
                tail = other[:, 1024:1152]
                mean_square = (squares + tail[:, 0:1] + tail[:, 64:65]) / D
                scale = lax.rsqrt(mean_square + norm_eps)
            both = (acc[h] + other[:, 0:1024]) * scale
            gate, up = both[:, 0:HIDDEN], both[:, HIDDEN:2 * HIDDEN]
            activations.append((gate / (1.0 + jnp.exp(-gate)) * up).astype(bf16))
        activation = jnp.concatenate(activations, axis=1)

        @pl.when(t == 0)
        def _():
            for copy in weight_copies[9:13]:
                copy.wait()
            for i in range(2, 6):
                wait_other(i)

        def send_six(xc, i):
            q = col_at(i)
            return remote(
                s6.at[xc, q], r6.at[x_chip, c], send6.at[xc, i], recv6.at[x_chip, c],
                (s, 2 * xc + core, q),
            )

        def down_step(j, _):
            xc = chip_at(CHIPS - 1 - j)
            first = pl.multiple_of(xc * WIDE, WIDE)
            columns = wd[:, :, pl.ds(first, WIDE)].reshape(2 * HIDDEN, WIDE)
            part = jnp.dot(activation, columns, preferred_element_type=f32)
            s6[xc] = part.astype(bf16).reshape(COLS, SUB, WIDE)
            for i in (2, 1, 3):
                send_six(xc, i).start()

            @pl.when(xc != x_chip)
            def _():
                send_six(xc, 0).start()

            return 0

        lax.fori_loop(0, CHIPS, down_step, 0)

        def sum_step(j, total):
            xc = chip_at(j)
            for i in (1, 3, 2):
                q = col_at(i)
                remote(
                    s6.at[xc, q], r6.at[xc, q], send6.at[xc, i], recv6.at[xc, q],
                    (s, pair, c),
                ).wait_recv()
                total = total + r6[xc, q].astype(f32)
            return total

        total = sum_step(0, after + s6[x_chip, c].astype(f32))

        def far_step(j, total):
            xc = chip_at(j)
            remote(
                s6.at[xc, c], r6.at[xc, c], send6.at[xc, 0], recv6.at[xc, c], (s, pair, c)
            ).wait_recv()
            return sum_step(j, total + r6[xc, c].astype(f32))

        total = lax.fori_loop(1, CHIPS, far_step, total)
        x_send[...] = total.astype(bf16)

        def send_one(i):
            return remote(
                x_send, xin.at[t + 1, c], send1.at[i], recv1.at[t, c],
                (s_next, r, col_at(i)),
            )

        def wait_one(i):
            return remote(
                x_send, xin.at[t + 1, col_at(i)], send1.at[i], recv1.at[t, col_at(i)],
                (s_next, r, col_at(i)),
            )

        @pl.when(t == 0)
        def _():
            pl.semaphore_wait(zready, 1)

        for i in (2, 1, 3, 0):
            send_one(i).start()

        for g in range(KVSPLIT):
            for i in range(1, ROWS):
                send_two(g, i).wait_send()
                send_three(g, i).wait_send()
        for i in range(1, COLS):
            send_four(i).wait_send()

        for i in range(1, PEERS):
            send_five(i).wait_send()
        for h in range(2):
            swap(h).wait_send()
        for i in range(CHIPS):
            for k in range(1, COLS):
                send_six(i, k).wait_send()

            @pl.when(i != x_chip)
            def _():
                send_six(i, 0).wait_send()

        for i in range(COLS):
            send_one(i).wait_send()
        for i in range(COLS):
            wait_one(i).wait_recv()
        return 0

    lax.fori_loop(0, TURNS, turn, 0)

    final = xin[TURNS].reshape(STREAMS, WIDE).astype(f32)
    final = pltpu.roll(final, lax.rem(WIDE - c * PIECE, WIDE), 1)
    out_ref[0] = final[:, 0:PIECE].astype(bf16)
    for i in range(1, COLS):
        send_init(i).wait_send()
    for i in (2, 4, 6):
        send_gain(i).wait_send()
    for copy in other_copies:
        copy.wait_send()


def per_device(
    hidden,
    lengths,
    attn_gain,
    ffn_gain,
    q_weight,
    key_weight,
    value_weight,
    out_weight,
    gate_weight,
    up_weight,
    down_weight,
    key_cache,
    value_cache,
):
    vmem = pl.BlockSpec(memory_space=pltpu.VMEM)
    hbm = pl.BlockSpec(memory_space=pl.ANY)
    dma = pltpu.SemaphoreType.DMA
    return pl.pallas_call(
        kernel,
        out_shape=jax.ShapeDtypeStruct((1, STREAMS, PIECE), bf16),
        in_specs=[hbm] * 13,
        out_specs=vmem,
        scratch_shapes=[
            pltpu.SMEM((TURNS, LOCAL), jnp.int32),
            pltpu.VMEM((1, STREAMS, PIECE), bf16),
            pltpu.VMEM((1, PIECE), bf16),
            pltpu.VMEM((1, PIECE), bf16),
            pltpu.VMEM((WIDE, KVSPLIT * QKV), bf16),
            pltpu.VMEM((1280, WIDE), bf16),
            pltpu.VMEM((2, CHIPS, WIDE, 2 * HIDDEN), bf16),
            pltpu.VMEM((2, HIDDEN, CHIPS * WIDE), bf16),
            pltpu.VMEM((TURNS, 2, LOCAL, CTX, HD), bf16),
            pltpu.VMEM((TURNS, 2, LOCAL, CTX, HD), bf16),
            pltpu.VMEM((COLS, 80, 256), bf16),
            pltpu.VMEM((1, WIDE), f32),
            pltpu.VMEM((ROWS, 8, WIDE), f32),
            pltpu.VMEM((TURNS, LOCAL, LOCAL * CTX), f32),
            pltpu.VMEM((TURNS + 1, COLS, SUB, WIDE), bf16),
            pltpu.VMEM((KVSPLIT, ROWS, SUB, PACK), bf16),
            pltpu.VMEM((KVSPLIT, ROWS, SUB, PACK), bf16),
            pltpu.VMEM((KVSPLIT, ROWS, SUB, OPACK), bf16),
            pltpu.VMEM((COLS, SUB, WIDE), bf16),
            pltpu.VMEM((COLS, SUB, WIDE), bf16),
            pltpu.VMEM((CHIPS, COLS, SUB, WIDE), bf16),
            pltpu.VMEM((2, STREAMS, 2 * HIDDEN), f32),
            pltpu.VMEM((2, STREAMS, 2 * HIDDEN + 128), bf16),
            pltpu.VMEM((2, STREAMS, 2 * HIDDEN + 128), bf16),
            pltpu.VMEM((CHIPS, COLS, SUB, WIDE), bf16),
            pltpu.VMEM((CHIPS, COLS, SUB, WIDE), bf16),
            pltpu.VMEM((SUB, WIDE), bf16),
            dma((4,)),
            dma((13,)),
            dma((TURNS, 4)),
            pltpu.SemaphoreType.REGULAR,
            dma((COLS,)),
            dma((COLS,)),
            dma((ROWS,)),
            dma((ROWS,)),
            dma((COLS,)),
            dma((TURNS, COLS)),
            dma((KVSPLIT, ROWS)),
            dma((KVSPLIT, ROWS)),
            dma((KVSPLIT, ROWS)),
            dma((KVSPLIT, ROWS)),
            dma((COLS,)),
            dma((COLS,)),
            dma((PEERS,)),
            dma((CHIPS, COLS)),
            dma((2,)),
            dma((2,)),
            dma((6,)),
            dma((6,)),
            dma((CHIPS, COLS)),
            dma((CHIPS, COLS)),
        ],
        compiler_params=pltpu.CompilerParams(
            collective_id=0, has_side_effects=True, vmem_limit_bytes=56 * 1024 * 1024
        ),
        cost_estimate=pl.CostEstimate(
            flops=TURNS * 2 * STREAMS * 9830400, bytes_accessed=24_000_000, transcendentals=0
        ),
    )(
        lengths,
        hidden,
        attn_gain,
        ffn_gain,
        q_weight,
        key_weight,
        value_weight,
        out_weight,
        gate_weight.reshape(CHIPS, 2, WIDE, HIDDEN),
        up_weight.reshape(CHIPS, 2, WIDE, HIDDEN),
        down_weight,
        key_cache,
        value_cache,
    )


def solution(mesh):
    return jax.shard_map(
        per_device,
        mesh=mesh,
        in_specs=(
            P("section", None, ("row", "col")),
            P(None, "row"),
            P("section", ("row", "col")),
            P("section", ("row", "col")),
            P("section", "row", "col"),
            P("section", "row", "col"),
            P("section", "row", "col"),
            P("section", "col", "row"),
            P("section", None, ("row", "col")),
            P("section", None, ("row", "col")),
            P("section", ("row", "col"), None),
            P("section", None, "row", "col", None, None),
            P("section", None, "row", "col", None, None),
        ),
        out_specs=P("section", None, ("row", "col")),
        check_vma=False,
    )
```

```python
import functools
import math

import jax
import jax.numpy as jnp
from jax import lax
from jax.experimental import pallas as pl
from jax.experimental.pallas import tpu as pltpu
from jax.sharding import PartitionSpec as P

D = 5120
HD = 128
CTX = 96
TURNS = 4
ROWS = 8
COLS = 4
CHIPS = 4
PEERS = 16
WIDE = 640
PIECE = 160
SUB = 16
STREAMS = 64
LOCAL = 8
KVSPLIT = 2
QKV = 896
PACK = 512
OPACK = 384
HIDDEN = 512
norm_eps = 1e-06
masked_score = -1e30
f32 = jnp.float32
bf16 = jnp.bfloat16


def remote(src, dst, send, recv, device):
    return pltpu.make_async_remote_copy(
        src_ref=src,
        dst_ref=dst,
        send_sem=send,
        recv_sem=recv,
        device_id=device,
        device_id_type=pl.DeviceIdType.MESH,
    )


def kernel(
    len_hbm,
    hid_hbm,
    ag_hbm,
    fg_hbm,
    wq_hbm,
    wk_hbm,
    wv_hbm,
    wo_hbm,
    wg_hbm,
    wu_hbm,
    wd_hbm,
    kc_hbm,
    vc_hbm,
    out_ref,
    len_ref,
    hid_ref,
    ag_ref,
    fg_ref,
    wqkv,
    wo,
    wgu,
    wd,
    kc,
    vc,
    init,
    gain1,
    gain2,
    bias,
    xin,
    s2,
    r2,
    o3,
    s4,
    r4,
    x2_all,
    acc,
    mine,
    theirs,
    s6,
    r6,
    x_send,
    isem,
    wsem,
    csem,
    zready,
    send0,
    recv0,
    sendg,
    recvg,
    send1,
    recv1,
    send2,
    recv2,
    send3,
    recv3,
    send4,
    recv4,
    send5,
    recv5,
    send_p,
    recv_p,
    send_w,
    recv_w,
    send6,
    recv6,
):
    s = lax.axis_index("section")
    r = lax.axis_index("row")
    c = lax.axis_index("col")
    x_chip = r // 2
    core = lax.rem(r, 2)
    pair = 2 * x_chip + 1 - core
    s_next = lax.rem(s + 1, TURNS)
    s_prev = lax.rem(s + TURNS - 1, TURNS)

    def row_at(i):
        return lax.rem(r + i, ROWS)

    def col_at(i):
        return lax.rem(c + i, COLS)

    inputs = [
        pltpu.make_async_copy(hid_hbm, hid_ref, isem.at[0]),
        pltpu.make_async_copy(ag_hbm, ag_ref, isem.at[1]),
        pltpu.make_async_copy(fg_hbm, fg_ref, isem.at[2]),
        pltpu.make_async_copy(len_hbm, len_ref, isem.at[3]),
    ]
    weight_copies = []
    for g in range(KVSPLIT):
        for source, first, width in ((wq_hbm, 0, WIDE), (wk_hbm, WIDE, HD), (wv_hbm, WIDE + HD, HD)):
            weight_copies.append(
                pltpu.make_async_copy(
                    source.at[0, :, pl.ds(g * width, width)],
                    wqkv.at[:, pl.ds(g * QKV + first, width)],
                    wsem.at[len(weight_copies)],
                )
            )
    weight_copies += [
        pltpu.make_async_copy(wo_hbm.at[0], wo, wsem.at[6]),
        pltpu.make_async_copy(
            wg_hbm.at[:, core], wgu.at[core, :, :, pl.ds(0, HIDDEN)], wsem.at[7]
        ),
        pltpu.make_async_copy(
            wu_hbm.at[:, core], wgu.at[core, :, :, pl.ds(HIDDEN, HIDDEN)], wsem.at[8]
        ),
    ]
    other_copies = [
        remote(
            wg_hbm.at[:, 1 - core], wgu.at[core, :, :, pl.ds(0, HIDDEN)],
            send_w.at[0], recv_w.at[0], (s, pair, c),
        ),
        remote(
            wu_hbm.at[:, 1 - core], wgu.at[core, :, :, pl.ds(HIDDEN, HIDDEN)],
            send_w.at[1], recv_w.at[1], (s, pair, c),
        ),
    ]
    for i in range(CHIPS):
        ours = pl.multiple_of((2 * i + core) * WIDE, WIDE)
        other = pl.multiple_of((2 * i + 1 - core) * WIDE, WIDE)
        weight_copies.append(
            pltpu.make_async_copy(
                wd_hbm.at[0, :, pl.ds(ours, WIDE)],
                wd.at[core, :, pl.ds(i * WIDE, WIDE)],
                wsem.at[9 + i],
            )
        )
        other_copies.append(
            remote(
                wd_hbm.at[0, :, pl.ds(other, WIDE)], wd.at[core, :, pl.ds(i * WIDE, WIDE)],
                send_w.at[2 + i], recv_w.at[2 + i], (s, pair, c),
            )
        )

    def wait_other(i):
        if i < 2:
            place = wgu.at[1 - core, :, :, pl.ds(i * HIDDEN, HIDDEN)]
        else:
            place = wd.at[1 - core, :, pl.ds((i - 2) * WIDE, WIDE)]
        remote(place, place, send_w.at[i], recv_w.at[i], (s, pair, c)).wait_recv()

    def cache_copies(t):
        m = lax.rem(s + TURNS - t, TURNS)
        copies = []
        for g in range(2):
            copies.append(
                pltpu.make_async_copy(kc_hbm.at[0, m, :, g], kc.at[t, g], csem.at[t, g])
            )
            copies.append(
                pltpu.make_async_copy(vc_hbm.at[0, m, :, g], vc.at[t, g], csem.at[t, 2 + g])
            )
        return copies

    barrier = pltpu.get_barrier_semaphore()
    greeted = [(s, row_at(i), c) for i in range(1, ROWS)]
    greeted += [(s, r, col_at(i)) for i in range(1, COLS)]
    greeted += [(s_prev, r, c), (s_next, r, c)]
    for device in greeted:
        pl.semaphore_signal(
            barrier, inc=1, device_id=device, device_id_type=pl.DeviceIdType.MESH
        )

    def row_of(dx):
        return 2 * lax.rem(x_chip + dx, CHIPS) + core

    for copy in inputs + weight_copies[:6]:
        copy.start()
    for copy in cache_copies(0):
        copy.start()
    for copy in weight_copies[6:]:
        copy.start()
    for t in range(1, TURNS):
        for copy in cache_copies(t):
            copy.start()
    for copy in inputs:
        copy.wait()

    init[c] = jnp.zeros((80, 256), bf16)
    init[c, 0:64, 0:PIECE] = hid_ref[0]
    gain_row = lax.broadcasted_iota(jnp.int32, (SUB, PIECE), 0)
    init[c, 64:80, 0:PIECE] = jnp.where(
        gain_row == 0, ag_ref[...].astype(f32), fg_ref[...].astype(f32)
    ).astype(bf16)

    pl.semaphore_wait(barrier, len(greeted))

    def send_init(i):
        return remote(
            init.at[c], init.at[c], send0.at[i], recv0.at[c], (s, r, col_at(i))
        )

    def wait_init(i):
        return remote(
            init.at[col_at(i)], init.at[col_at(i)], send0.at[i], recv0.at[col_at(i)],
            (s, r, col_at(i)),
        )

    for i in (2, 1, 3):
        send_init(i).start()
    for copy in other_copies[:1]:
        copy.start()
    stream_row = lax.broadcasted_iota(jnp.int32, (LOCAL, LOCAL * CTX), 0)
    position = lax.broadcasted_iota(jnp.int32, (LOCAL, LOCAL * CTX), 1)
    for t in range(TURNS):
        m = lax.rem(s + TURNS - t, TURNS)
        offsets = jnp.full((LOCAL, LOCAL * CTX), masked_score, f32)
        for b in range(LOCAL):
            live = (
                (stream_row == b)
                & (position >= b * CTX)
                & (position < b * CTX + len_ref[m, b])
            )
            offsets = jnp.where(live, 0.0, offsets)
        bias[t] = offsets

    for i in range(1, COLS):
        wait_init(i).wait_recv()
    pl.semaphore_signal(
        zready, inc=1, device_id=(s_prev, r, c), device_id_type=pl.DeviceIdType.MESH
    )
    joined = None
    for i in range(COLS):
        piece = jnp.concatenate(
            [init[i].astype(f32), jnp.zeros((80, WIDE - 256), f32)], axis=1
        )
        if i:
            piece = pltpu.roll(piece, i * PIECE, 1)
        joined = piece if joined is None else joined + piece
    xin[0] = joined[0:64].astype(bf16).reshape(COLS, SUB, WIDE)
    gain1[...] = joined[64:65]
    gain2[r] = jnp.broadcast_to(joined[65:66], (8, WIDE))

    def send_gain(i):
        return remote(
            gain2.at[r], gain2.at[r], sendg.at[i], recvg.at[r], (s, row_at(i), c)
        )

    def wait_gain(i):
        return remote(
            gain2.at[row_at(i)], gain2.at[row_at(i)], sendg.at[i], recvg.at[row_at(i)],
            (s, row_at(i), c),
        )

    def turn(t, _):
        x_all = xin[t].reshape(STREAMS, WIDE).astype(f32)
        squares = jnp.sum(x_all * x_all, axis=1, keepdims=True)
        high = squares.astype(bf16).astype(f32)
        low = squares - high
        left = (x_all * gain1[...]).astype(bf16)

        @pl.when(t == 0)
        def _():
            for copy in weight_copies[:6]:
                copy.wait()

        lane = lax.broadcasted_iota(jnp.int32, (STREAMS, 128), 1)
        sums = jnp.where(lane < 64, high, low).reshape(ROWS, LOCAL, 128)

        def send_two(g, i):
            return remote(
                s2.at[g, row_at(i)], r2.at[g, r], send2.at[g, i], recv2.at[g, r],
                (s, row_at(i), c),
            )

        def wait_two(g, i):
            return remote(
                s2.at[g, row_at(i)], r2.at[g, row_at(i)], send2.at[g, i],
                recv2.at[g, row_at(i)], (s, row_at(i), c),
            )

        for g in range(KVSPLIT):
            part = jnp.dot(
                left, wqkv[:, g * QKV:(g + 1) * QKV], preferred_element_type=f32
            ).reshape(ROWS, LOCAL, QKV)
            rest = jnp.concatenate([part[:, :, PACK:QKV], sums], axis=2)
            s2[g] = jnp.concatenate([part[:, :, 0:PACK], rest], axis=1).astype(bf16)
            for i in (4, 3, 5, 2, 6, 1, 7):
                send_two(g, i).start()

        @pl.when(t == 0)
        def _():
            for i in (2, 4, 6):
                send_gain(i).start()
            other_copies[1].start()

        @pl.when(t == 0)
        def _():
            for copy in cache_copies(0):
                copy.wait()

        @pl.when(t > 0)
        def _():
            for copy in cache_copies(t):
                copy.wait()

        def send_three(g, i):
            return remote(
                o3.at[g, r], o3.at[g, r], send3.at[g, i], recv3.at[g, r], (s, row_at(i), c)
            )

        def wait_three(g, i):
            return remote(
                o3.at[g, row_at(i)], o3.at[g, row_at(i)], send3.at[g, i],
                recv3.at[g, row_at(i)], (s, row_at(i), c),
            )

        score_scale = 1.0 / math.sqrt(HD)
        offsets = jnp.concatenate([bias[t]] * 5, axis=0)
        for g in range(KVSPLIT):
            total = s2[g, r].astype(f32)
            for i in (1, 7, 2, 6, 3, 5, 4):
                wait_two(g, i).wait_recv()
                total = total + r2[g, row_at(i)].astype(f32)
            top, bottom = total[0:8], total[8:16]
            mean_square = (bottom[:, 384:385] + bottom[:, 448:449]) / D
            scale = lax.rsqrt(mean_square + norm_eps)
            top = (top * scale).astype(bf16).astype(f32)
            bottom = (bottom[:, 0:384] * scale).astype(bf16).astype(f32)
            queries = jnp.concatenate(
                [top[:, j * HD:(j + 1) * HD] for j in range(4)] + [bottom[:, 0:HD]], axis=0
            )
            key_new = jnp.concatenate([bottom[:, HD:2 * HD]] * 5, axis=0)
            value_new = jnp.concatenate([bottom[:, 2 * HD:3 * HD]] * 5, axis=0)
            keys = kc[t, g].reshape(LOCAL * CTX, HD)
            values = vc[t, g].reshape(LOCAL * CTX, HD)
            scores = lax.dot_general(
                queries.astype(bf16), keys, (((1,), (1,)), ((), ())),
                preferred_element_type=f32,
            )
            scores = scores * score_scale + offsets
            self_score = jnp.sum(queries * key_new, axis=1, keepdims=True) * score_scale
            row_max = jnp.maximum(jnp.max(scores, axis=1, keepdims=True), self_score)
            weights = jnp.exp(scores - row_max)
            self_weight = jnp.exp(self_score - row_max)
            denominator = jnp.sum(weights, axis=1, keepdims=True) + self_weight
            share = 1.0 / denominator
            probs = (weights * share).astype(bf16)
            self_prob = (self_weight * share).astype(bf16).astype(f32)
            mixed = jnp.dot(probs, values, preferred_element_type=f32)
            mixed = mixed + self_prob * value_new
            heads = [mixed[j * 8:(j + 1) * 8] for j in range(5)]
            o3[g, r] = jnp.concatenate(
                [
                    jnp.concatenate(heads[0:3], axis=1),
                    jnp.concatenate(heads[3:5] + [jnp.zeros((LOCAL, HD), f32)], axis=1),
                ],
                axis=0,
            ).astype(bf16)
            for i in (4, 3, 5, 2, 6, 1, 7):
                send_three(g, i).start()

        @pl.when(t == 0)
        def _():
            weight_copies[6].wait()
            for copy in other_copies[2:]:
                copy.start()

        out_part = None
        for g in range(KVSPLIT):
            for i in (1, 7, 2, 6, 3, 5, 4):
                wait_three(g, i).wait_recv()
            gathered = o3[g].astype(f32)
            heads = jnp.concatenate(
                [
                    gathered[:, 0:8].reshape(STREAMS, OPACK),
                    gathered[:, 8:16, 0:WIDE - OPACK].reshape(STREAMS, WIDE - OPACK),
                ],
                axis=1,
            ).astype(bf16)
            product = jnp.dot(
                heads, wo[g * WIDE:(g + 1) * WIDE, :], preferred_element_type=f32
            )
            out_part = product if out_part is None else out_part + product
        s4[...] = out_part.astype(bf16).reshape(COLS, SUB, WIDE)

        def send_four(i):
            return remote(
                s4.at[col_at(i)], r4.at[c], send4.at[i], recv4.at[c], (s, r, col_at(i))
            )

        def wait_four(i):
            return remote(
                s4.at[col_at(i)], r4.at[col_at(i)], send4.at[i], recv4.at[col_at(i)],
                (s, r, col_at(i)),
            )

        for i in (2, 1, 3):
            send_four(i).start()
        after = xin[t, c].astype(f32) + s4[c].astype(f32)
        for i in (1, 3, 2):
            wait_four(i).wait_recv()
            after = after + r4[col_at(i)].astype(f32)
        x2_all[x_chip, c] = after.astype(bf16)
        after = x2_all[x_chip, c].astype(f32)

        def send_five(i):
            return remote(
                x2_all.at[x_chip, c], x2_all.at[x_chip, c], send5.at[i], recv5.at[x_chip, c],
                (s, row_of(i // COLS), col_at(i % COLS)),
            )

        for i in (2, 1, 3, 6, 14, 5, 7, 13, 15, 4, 12, 10, 9, 11, 8):
            send_five(i).start()

        @pl.when(t == 0)
        def _():
            for i in (2, 4, 6):
                wait_gain(i).wait_recv()
            for copy in weight_copies[7:9]:
                copy.wait()
            for i in range(2):
                wait_other(i)

        def chip_at(j):
            return lax.rem(x_chip + j + (j // 2) * (5 - 2 * j), 4)

        def collect(xc, own):
            for i in (1, 3, 2) if own else (1, 3, 2, 0):
                q = col_at(i)
                remote(
                    x2_all.at[xc, q], x2_all.at[xc, q], send5.at[1], recv5.at[xc, q],
                    (s, pair, c),
                ).wait_recv()
            values = x2_all[xc].reshape(STREAMS, WIDE).astype(f32)
            square = values * values
            squares = square[:, 0:128]
            for k in range(1, 5):
                squares = squares + square[:, k * 128:(k + 1) * 128]
            return (values * gain2[2 * xc + core, 0:1]).astype(bf16), squares

        def gate_part(scaled, xc, h):
            return jnp.dot(scaled, wgu[h, xc], preferred_element_type=f32)

        scaled, squares = collect(x_chip, True)
        for h in range(2):
            acc[h] = gate_part(scaled, x_chip, h)

        def gate_step(j, squares):
            xc = chip_at(j)
            scaled, more = collect(xc, False)
            for h in range(2):
                acc[h] += gate_part(scaled, xc, h)
            return squares + more

        squares = lax.fori_loop(1, CHIPS - 1, gate_step, squares)

        def swap(h):
            return remote(
                mine.at[h], theirs.at[h], send_p.at[h], recv_p.at[h], (s, pair, c)
            )

        far = chip_at(CHIPS - 1)
        scaled, more = collect(far, False)
        squares = jnp.sum(squares + more, axis=1, keepdims=True)
        high = squares.astype(bf16).astype(f32)
        sums = jnp.where(lane < 64, high, squares - high)
        for h in range(2):
            product = acc[h] + gate_part(scaled, far, h)
            acc[h] = product
            mine[h] = jnp.concatenate([product, sums], axis=1).astype(bf16)
            swap(h).start()
        @pl.when(t == 0)
        def _():
            for copy in weight_copies[9:13]:
                copy.wait()
            for i in range(2, 6):
                wait_other(i)

        def down_columns(xc):
            return pl.ds(pl.multiple_of(xc * WIDE, WIDE), WIDE)

        activations = []
        for h in range(2):
            swap(h).wait_recv()
            other = theirs[h].astype(f32)
            if h == 0:
                tail = other[:, 1024:1152]
                mean_square = (squares + tail[:, 0:1] + tail[:, 64:65]) / D
                scale = lax.rsqrt(mean_square + norm_eps)
            both = (acc[h] + other[:, 0:1024]) * scale
            gate, up = both[:, 0:HIDDEN], both[:, HIDDEN:2 * HIDDEN]
            half = 0.5 * gate
            activations.append(((half + half * jnp.tanh(half)) * up).astype(bf16))
            if h == 0:
                far_part = jnp.dot(
                    activations[0], wd[0, :, down_columns(far)], preferred_element_type=f32
                )
        activation = jnp.concatenate(activations, axis=1)

        def send_six(xc, i):
            q = col_at(i)
            return remote(
                s6.at[xc, q], r6.at[x_chip, c], send6.at[xc, i], recv6.at[x_chip, c],
                (s, 2 * xc + core, q),
            )

        def send_part(xc, part):
            s6[xc] = part.astype(bf16).reshape(COLS, SUB, WIDE)
            for i in (2, 1, 3):
                send_six(xc, i).start()

            @pl.when(xc != x_chip)
            def _():
                send_six(xc, 0).start()

        def down_step(j, _):
            xc = lax.rem(x_chip + lax.rem(2 * j + 2, 4) + j // 2, CHIPS)
            columns = wd[:, :, down_columns(xc)].reshape(2 * HIDDEN, WIDE)
            send_part(xc, jnp.dot(activation, columns, preferred_element_type=f32))
            return 0

        far_part = far_part + jnp.dot(
            activations[1], wd[1, :, down_columns(far)], preferred_element_type=f32
        )
        send_part(far, far_part)
        lax.fori_loop(1, CHIPS, down_step, 0)

        def sum_step(j, total):
            xc = chip_at(j)
            for i in (1, 3, 2):
                q = col_at(i)
                remote(
                    s6.at[xc, q], r6.at[xc, q], send6.at[xc, i], recv6.at[xc, q],
                    (s, pair, c),
                ).wait_recv()
                total = total + r6[xc, q].astype(f32)
            return total

        total = sum_step(0, after + s6[x_chip, c].astype(f32))

        def far_step(j, total):
            xc = chip_at(j)
            remote(
                s6.at[xc, c], r6.at[xc, c], send6.at[xc, 0], recv6.at[xc, c], (s, pair, c)
            ).wait_recv()
            return sum_step(j, total + r6[xc, c].astype(f32))

        total = lax.fori_loop(1, CHIPS, far_step, total)
        x_send[...] = total.astype(bf16)

        def send_one(i):
            return remote(
                x_send, xin.at[t + 1, c], send1.at[i], recv1.at[t, c],
                (s_next, r, col_at(i)),
            )

        def wait_one(i):
            return remote(
                x_send, xin.at[t + 1, col_at(i)], send1.at[i], recv1.at[t, col_at(i)],
                (s_next, r, col_at(i)),
            )

        @pl.when(t == 0)
        def _():
            pl.semaphore_wait(zready, 1)

        for i in (2, 1, 3, 0):
            send_one(i).start()

        for g in range(KVSPLIT):
            for i in range(1, ROWS):
                send_two(g, i).wait_send()
                send_three(g, i).wait_send()
        for i in range(1, COLS):
            send_four(i).wait_send()

        for i in range(1, PEERS):
            send_five(i).wait_send()
        for h in range(2):
            swap(h).wait_send()
        for i in range(CHIPS):
            for k in range(1, COLS):
                send_six(i, k).wait_send()

            @pl.when(i != x_chip)
            def _():
                send_six(i, 0).wait_send()

        for i in range(COLS):
            send_one(i).wait_send()
        for i in range(COLS):
            wait_one(i).wait_recv()
        return 0

    lax.fori_loop(0, TURNS, turn, 0)

    final = xin[TURNS].reshape(STREAMS, WIDE).astype(f32)
    final = pltpu.roll(final, lax.rem(WIDE - c * PIECE, WIDE), 1)
    out_ref[0] = final[:, 0:PIECE].astype(bf16)
    for i in range(1, COLS):
        send_init(i).wait_send()
    for i in (2, 4, 6):
        send_gain(i).wait_send()
    for copy in other_copies:
        copy.wait_send()


def per_device(
    hidden,
    lengths,
    attn_gain,
    ffn_gain,
    q_weight,
    key_weight,
    value_weight,
    out_weight,
    gate_weight,
    up_weight,
    down_weight,
    key_cache,
    value_cache,
):
    vmem = pl.BlockSpec(memory_space=pltpu.VMEM)
    hbm = pl.BlockSpec(memory_space=pl.ANY)
    dma = pltpu.SemaphoreType.DMA
    return pl.pallas_call(
        kernel,
        out_shape=jax.ShapeDtypeStruct((1, STREAMS, PIECE), bf16),
        in_specs=[hbm] * 13,
        out_specs=vmem,
        scratch_shapes=[
            pltpu.SMEM((TURNS, LOCAL), jnp.int32),
            pltpu.VMEM((1, STREAMS, PIECE), bf16),
            pltpu.VMEM((1, PIECE), bf16),
            pltpu.VMEM((1, PIECE), bf16),
            pltpu.VMEM((WIDE, KVSPLIT * QKV), bf16),
            pltpu.VMEM((1280, WIDE), bf16),
            pltpu.VMEM((2, CHIPS, WIDE, 2 * HIDDEN), bf16),
            pltpu.VMEM((2, HIDDEN, CHIPS * WIDE), bf16),
            pltpu.VMEM((TURNS, 2, LOCAL, CTX, HD), bf16),
            pltpu.VMEM((TURNS, 2, LOCAL, CTX, HD), bf16),
            pltpu.VMEM((COLS, 80, 256), bf16),
            pltpu.VMEM((1, WIDE), f32),
            pltpu.VMEM((ROWS, 8, WIDE), f32),
            pltpu.VMEM((TURNS, LOCAL, LOCAL * CTX), f32),
            pltpu.VMEM((TURNS + 1, COLS, SUB, WIDE), bf16),
            pltpu.VMEM((KVSPLIT, ROWS, SUB, PACK), bf16),
            pltpu.VMEM((KVSPLIT, ROWS, SUB, PACK), bf16),
            pltpu.VMEM((KVSPLIT, ROWS, SUB, OPACK), bf16),
            pltpu.VMEM((COLS, SUB, WIDE), bf16),
            pltpu.VMEM((COLS, SUB, WIDE), bf16),
            pltpu.VMEM((CHIPS, COLS, SUB, WIDE), bf16),
            pltpu.VMEM((2, STREAMS, 2 * HIDDEN), f32),
            pltpu.VMEM((2, STREAMS, 2 * HIDDEN + 128), bf16),
            pltpu.VMEM((2, STREAMS, 2 * HIDDEN + 128), bf16),
            pltpu.VMEM((CHIPS, COLS, SUB, WIDE), bf16),
            pltpu.VMEM((CHIPS, COLS, SUB, WIDE), bf16),
            pltpu.VMEM((SUB, WIDE), bf16),
            dma((4,)),
            dma((13,)),
            dma((TURNS, 4)),
            pltpu.SemaphoreType.REGULAR,
            dma((COLS,)),
            dma((COLS,)),
            dma((ROWS,)),
            dma((ROWS,)),
            dma((COLS,)),
            dma((TURNS, COLS)),
            dma((KVSPLIT, ROWS)),
            dma((KVSPLIT, ROWS)),
            dma((KVSPLIT, ROWS)),
            dma((KVSPLIT, ROWS)),
            dma((COLS,)),
            dma((COLS,)),
            dma((PEERS,)),
            dma((CHIPS, COLS)),
            dma((2,)),
            dma((2,)),
            dma((6,)),
            dma((6,)),
            dma((CHIPS, COLS)),
            dma((CHIPS, COLS)),
        ],
        compiler_params=pltpu.CompilerParams(
            collective_id=0, has_side_effects=True, vmem_limit_bytes=56 * 1024 * 1024
        ),
        cost_estimate=pl.CostEstimate(
            flops=TURNS * 2 * STREAMS * 9830400, bytes_accessed=24_000_000, transcendentals=0
        ),
    )(
        lengths,
        hidden,
        attn_gain,
        ffn_gain,
        q_weight,
        key_weight,
        value_weight,
        out_weight,
        gate_weight.reshape(CHIPS, 2, WIDE, HIDDEN),
        up_weight.reshape(CHIPS, 2, WIDE, HIDDEN),
        down_weight,
        key_cache,
        value_cache,
    )


def solution(mesh):
    return jax.shard_map(
        per_device,
        mesh=mesh,
        in_specs=(
            P("section", None, ("row", "col")),
            P(None, "row"),
            P("section", ("row", "col")),
            P("section", ("row", "col")),
            P("section", "row", "col"),
            P("section", "row", "col"),
            P("section", "row", "col"),
            P("section", "col", "row"),
            P("section", None, ("row", "col")),
            P("section", None, ("row", "col")),
            P("section", ("row", "col"), None),
            P("section", None, "row", "col", None, None),
            P("section", None, "row", "col", None, None),
        ),
        out_specs=P("section", None, ("row", "col")),
        check_vma=False,
    )
```

```python
import functools
import math

import jax
import jax.numpy as jnp
from jax import lax
from jax.experimental import pallas as pl
from jax.experimental.pallas import tpu as pltpu
from jax.sharding import PartitionSpec as P

D = 5120
HD = 128
CTX = 96
TURNS = 4
ROWS = 8
COLS = 4
CHIPS = 4
PEERS = 16
WIDE = 640
PIECE = 160
SUB = 16
STREAMS = 64
LOCAL = 8
KVSPLIT = 2
QKV = 896
PACK = 512
OPACK = 384
HIDDEN = 512
norm_eps = 1e-06
masked_score = -1e30
f32 = jnp.float32
bf16 = jnp.bfloat16


def remote(src, dst, send, recv, device):
    return pltpu.make_async_remote_copy(
        src_ref=src,
        dst_ref=dst,
        send_sem=send,
        recv_sem=recv,
        device_id=device,
        device_id_type=pl.DeviceIdType.MESH,
    )


def kernel(
    len_hbm,
    hid_hbm,
    ag_hbm,
    fg_hbm,
    wq_hbm,
    wk_hbm,
    wv_hbm,
    wo_hbm,
    wg_hbm,
    wu_hbm,
    wd_hbm,
    kc_hbm,
    vc_hbm,
    out_ref,
    len_ref,
    hid_ref,
    ag_ref,
    fg_ref,
    wqkv,
    wo,
    wgu,
    wd,
    kc,
    vc,
    init,
    gain1,
    gain2,
    bias,
    xin,
    s2,
    r2,
    o3,
    s4,
    r4,
    x2_all,
    acc,
    mine,
    theirs,
    s6,
    r6,
    x_send,
    isem,
    wsem,
    csem,
    zready,
    send0,
    recv0,
    sendg,
    recvg,
    send1,
    recv1,
    send2,
    recv2,
    send3,
    recv3,
    send4,
    recv4,
    send5,
    recv5,
    send_p,
    recv_p,
    send_w,
    recv_w,
    send6,
    recv6,
):
    s = lax.axis_index("section")
    r = lax.axis_index("row")
    c = lax.axis_index("col")
    x_chip = r // 2
    core = lax.rem(r, 2)
    pair = 2 * x_chip + 1 - core
    s_next = lax.rem(s + 1, TURNS)
    s_prev = lax.rem(s + TURNS - 1, TURNS)

    def row_at(i):
        return lax.rem(r + i, ROWS)

    def col_at(i):
        return lax.rem(c + i, COLS)

    inputs = [
        pltpu.make_async_copy(hid_hbm, hid_ref, isem.at[0]),
        pltpu.make_async_copy(ag_hbm, ag_ref, isem.at[1]),
        pltpu.make_async_copy(fg_hbm, fg_ref, isem.at[2]),
        pltpu.make_async_copy(len_hbm, len_ref, isem.at[3]),
    ]
    weight_copies = []
    for g in range(KVSPLIT):
        for source, first, width in ((wq_hbm, 0, WIDE), (wk_hbm, WIDE, HD), (wv_hbm, WIDE + HD, HD)):
            weight_copies.append(
                pltpu.make_async_copy(
                    source.at[0, :, pl.ds(g * width, width)],
                    wqkv.at[:, pl.ds(g * QKV + first, width)],
                    wsem.at[len(weight_copies)],
                )
            )
    weight_copies += [
        pltpu.make_async_copy(wo_hbm.at[0], wo, wsem.at[6]),
        pltpu.make_async_copy(
            wg_hbm.at[:, core], wgu.at[core, :, :, pl.ds(0, HIDDEN)], wsem.at[7]
        ),
        pltpu.make_async_copy(
            wu_hbm.at[:, core], wgu.at[core, :, :, pl.ds(HIDDEN, HIDDEN)], wsem.at[8]
        ),
    ]
    other_copies = [
        remote(
            wg_hbm.at[:, 1 - core], wgu.at[core, :, :, pl.ds(0, HIDDEN)],
            send_w.at[0], recv_w.at[0], (s, pair, c),
        ),
        remote(
            wu_hbm.at[:, 1 - core], wgu.at[core, :, :, pl.ds(HIDDEN, HIDDEN)],
            send_w.at[1], recv_w.at[1], (s, pair, c),
        ),
    ]
    for i in range(CHIPS):
        ours = pl.multiple_of((2 * i + core) * WIDE, WIDE)
        other = pl.multiple_of((2 * i + 1 - core) * WIDE, WIDE)
        weight_copies.append(
            pltpu.make_async_copy(
                wd_hbm.at[0, :, pl.ds(ours, WIDE)],
                wd.at[core, :, pl.ds(i * WIDE, WIDE)],
                wsem.at[9 + i],
            )
        )
        other_copies.append(
            remote(
                wd_hbm.at[0, :, pl.ds(other, WIDE)], wd.at[core, :, pl.ds(i * WIDE, WIDE)],
                send_w.at[2 + i], recv_w.at[2 + i], (s, pair, c),
            )
        )

    def wait_other(i):
        if i < 2:
            place = wgu.at[1 - core, :, :, pl.ds(i * HIDDEN, HIDDEN)]
        else:
            place = wd.at[1 - core, :, pl.ds((i - 2) * WIDE, WIDE)]
        remote(place, place, send_w.at[i], recv_w.at[i], (s, pair, c)).wait_recv()

    def cache_copies(t):
        m = lax.rem(s + TURNS - t, TURNS)
        copies = []
        for g in range(2):
            copies.append(
                pltpu.make_async_copy(kc_hbm.at[0, m, :, g], kc.at[t, g], csem.at[t, g])
            )
            copies.append(
                pltpu.make_async_copy(vc_hbm.at[0, m, :, g], vc.at[t, g], csem.at[t, 2 + g])
            )
        return copies

    barrier = pltpu.get_barrier_semaphore()
    greeted = [(s, row_at(i), c) for i in range(1, ROWS)]
    greeted += [(s, r, col_at(i)) for i in range(1, COLS)]
    greeted += [(s_prev, r, c), (s_next, r, c)]
    for device in greeted:
        pl.semaphore_signal(
            barrier, inc=1, device_id=device, device_id_type=pl.DeviceIdType.MESH
        )

    def row_of(dx):
        return 2 * lax.rem(x_chip + dx, CHIPS) + core

    for copy in inputs + weight_copies[:6]:
        copy.start()
    for copy in cache_copies(0):
        copy.start()
    for copy in weight_copies[6:]:
        copy.start()
    for t in range(1, TURNS):
        for copy in cache_copies(t):
            copy.start()
    for copy in inputs:
        copy.wait()

    init[c] = jnp.zeros((80, 256), bf16)
    init[c, 0:64, 0:PIECE] = hid_ref[0]
    gain_row = lax.broadcasted_iota(jnp.int32, (SUB, PIECE), 0)
    init[c, 64:80, 0:PIECE] = jnp.where(
        gain_row == 0, ag_ref[...].astype(f32), fg_ref[...].astype(f32)
    ).astype(bf16)

    pl.semaphore_wait(barrier, len(greeted))

    def send_init(i):
        return remote(
            init.at[c], init.at[c], send0.at[i], recv0.at[c], (s, r, col_at(i))
        )

    def wait_init(i):
        return remote(
            init.at[col_at(i)], init.at[col_at(i)], send0.at[i], recv0.at[col_at(i)],
            (s, r, col_at(i)),
        )

    for i in (2, 1, 3):
        send_init(i).start()
    for copy in other_copies[:1]:
        copy.start()
    stream_row = lax.broadcasted_iota(jnp.int32, (LOCAL, LOCAL * CTX), 0)
    position = lax.broadcasted_iota(jnp.int32, (LOCAL, LOCAL * CTX), 1)
    for t in range(TURNS):
        m = lax.rem(s + TURNS - t, TURNS)
        offsets = jnp.full((LOCAL, LOCAL * CTX), masked_score, f32)
        for b in range(LOCAL):
            live = (
                (stream_row == b)
                & (position >= b * CTX)
                & (position < b * CTX + len_ref[m, b])
            )
            offsets = jnp.where(live, 0.0, offsets)
        bias[t] = offsets

    for i in range(1, COLS):
        wait_init(i).wait_recv()
    pl.semaphore_signal(
        zready, inc=1, device_id=(s_prev, r, c), device_id_type=pl.DeviceIdType.MESH
    )
    joined = None
    for i in range(COLS):
        piece = jnp.concatenate(
            [init[i].astype(f32), jnp.zeros((80, WIDE - 256), f32)], axis=1
        )
        if i:
            piece = pltpu.roll(piece, i * PIECE, 1)
        joined = piece if joined is None else joined + piece
    xin[0] = joined[0:64].astype(bf16).reshape(COLS, SUB, WIDE)
    gain1[...] = joined[64:65]
    gain2[r] = jnp.broadcast_to(joined[65:66], (8, WIDE))

    def send_gain(i):
        return remote(
            gain2.at[r], gain2.at[r], sendg.at[i], recvg.at[r], (s, row_at(i), c)
        )

    def wait_gain(i):
        return remote(
            gain2.at[row_at(i)], gain2.at[row_at(i)], sendg.at[i], recvg.at[row_at(i)],
            (s, row_at(i), c),
        )

    def turn(t, _):
        x_all = xin[t].reshape(STREAMS, WIDE).astype(f32)
        squares = jnp.sum(x_all * x_all, axis=1, keepdims=True)
        high = squares.astype(bf16).astype(f32)
        low = squares - high
        left = (x_all * gain1[...]).astype(bf16)

        @pl.when(t == 0)
        def _():
            for copy in weight_copies[:6]:
                copy.wait()

        lane = lax.broadcasted_iota(jnp.int32, (STREAMS, 128), 1)
        sums = jnp.where(lane < 64, high, low).reshape(ROWS, LOCAL, 128)

        def send_two(g, i):
            return remote(
                s2.at[g, row_at(i)], r2.at[g, r], send2.at[g, i], recv2.at[g, r],
                (s, row_at(i), c),
            )

        def wait_two(g, i):
            return remote(
                s2.at[g, row_at(i)], r2.at[g, row_at(i)], send2.at[g, i],
                recv2.at[g, row_at(i)], (s, row_at(i), c),
            )

        for g in range(KVSPLIT):
            part = jnp.dot(
                left, wqkv[:, g * QKV:(g + 1) * QKV], preferred_element_type=f32
            ).reshape(ROWS, LOCAL, QKV)
            rest = jnp.concatenate([part[:, :, PACK:QKV], sums], axis=2)
            s2[g] = jnp.concatenate([part[:, :, 0:PACK], rest], axis=1).astype(bf16)
            for i in (4, 3, 5, 2, 6, 1, 7):
                send_two(g, i).start()

        @pl.when(t == 0)
        def _():
            for i in (2, 4, 6):
                send_gain(i).start()
            other_copies[1].start()

        @pl.when(t == 0)
        def _():
            for copy in cache_copies(0):
                copy.wait()

        @pl.when(t > 0)
        def _():
            for copy in cache_copies(t):
                copy.wait()

        def send_three(g, i):
            return remote(
                o3.at[g, r], o3.at[g, r], send3.at[g, i], recv3.at[g, r], (s, row_at(i), c)
            )

        def wait_three(g, i):
            return remote(
                o3.at[g, row_at(i)], o3.at[g, row_at(i)], send3.at[g, i],
                recv3.at[g, row_at(i)], (s, row_at(i), c),
            )

        score_scale = 1.0 / math.sqrt(HD)
        offsets = jnp.concatenate([bias[t]] * 5, axis=0)
        for g in range(KVSPLIT):
            total = s2[g, r].astype(f32)
            for i in (1, 7, 2, 6, 3, 5, 4):
                wait_two(g, i).wait_recv()
                total = total + r2[g, row_at(i)].astype(f32)
            top, bottom = total[0:8], total[8:16]
            mean_square = (bottom[:, 384:385] + bottom[:, 448:449]) / D
            scale = lax.rsqrt(mean_square + norm_eps)
            top = (top * scale).astype(bf16).astype(f32)
            bottom = (bottom[:, 0:384] * scale).astype(bf16).astype(f32)
            queries = jnp.concatenate(
                [top[:, j * HD:(j + 1) * HD] for j in range(4)] + [bottom[:, 0:HD]], axis=0
            )
            key_new = jnp.concatenate([bottom[:, HD:2 * HD]] * 5, axis=0)
            value_new = jnp.concatenate([bottom[:, 2 * HD:3 * HD]] * 5, axis=0)
            keys = kc[t, g].reshape(LOCAL * CTX, HD)
            values = vc[t, g].reshape(LOCAL * CTX, HD)
            scores = lax.dot_general(
                queries.astype(bf16), keys, (((1,), (1,)), ((), ())),
                preferred_element_type=f32,
            )
            scores = scores * score_scale + offsets
            self_score = jnp.sum(queries * key_new, axis=1, keepdims=True) * score_scale
            row_max = jnp.maximum(jnp.max(scores, axis=1, keepdims=True), self_score)
            weights = jnp.exp(scores - row_max)
            self_weight = jnp.exp(self_score - row_max)
            denominator = jnp.sum(weights, axis=1, keepdims=True) + self_weight
            share = 1.0 / denominator
            probs = (weights * share).astype(bf16)
            self_prob = (self_weight * share).astype(bf16).astype(f32)
            mixed = jnp.dot(probs, values, preferred_element_type=f32)
            mixed = mixed + self_prob * value_new
            heads = [mixed[j * 8:(j + 1) * 8] for j in range(5)]
            o3[g, r] = jnp.concatenate(
                [
                    jnp.concatenate(heads[0:3], axis=1),
                    jnp.concatenate(heads[3:5] + [jnp.zeros((LOCAL, HD), f32)], axis=1),
                ],
                axis=0,
            ).astype(bf16)
            for i in (4, 3, 5, 2, 6, 1, 7):
                send_three(g, i).start()

        @pl.when(t == 0)
        def _():
            weight_copies[6].wait()
            for copy in other_copies[2:]:
                copy.start()

        out_part = None
        for g in range(KVSPLIT):
            for i in (1, 7, 2, 6, 3, 5, 4):
                wait_three(g, i).wait_recv()
            gathered = o3[g].astype(f32)
            heads = jnp.concatenate(
                [
                    gathered[:, 0:8].reshape(STREAMS, OPACK),
                    gathered[:, 8:16, 0:WIDE - OPACK].reshape(STREAMS, WIDE - OPACK),
                ],
                axis=1,
            ).astype(bf16)
            product = jnp.dot(
                heads, wo[g * WIDE:(g + 1) * WIDE, :], preferred_element_type=f32
            )
            out_part = product if out_part is None else out_part + product
        s4[...] = out_part.astype(bf16).reshape(COLS, SUB, WIDE)

        def send_four(i):
            return remote(
                s4.at[col_at(i)], r4.at[c], send4.at[i], recv4.at[c], (s, r, col_at(i))
            )

        def wait_four(i):
            return remote(
                s4.at[col_at(i)], r4.at[col_at(i)], send4.at[i], recv4.at[col_at(i)],
                (s, r, col_at(i)),
            )

        for i in (2, 1, 3):
            send_four(i).start()
        after = xin[t, c].astype(f32) + s4[c].astype(f32)
        for i in (1, 3, 2):
            wait_four(i).wait_recv()
            after = after + r4[col_at(i)].astype(f32)
        x2_all[x_chip, c] = after.astype(bf16)
        after = x2_all[x_chip, c].astype(f32)

        def send_five(i):
            return remote(
                x2_all.at[x_chip, c], x2_all.at[x_chip, c], send5.at[i], recv5.at[x_chip, c],
                (s, row_of(i // COLS), col_at(i % COLS)),
            )

        for i in (2, 1, 3, 6, 14, 5, 7, 13, 15, 4, 12, 10, 9, 11, 8):
            send_five(i).start()

        @pl.when(t == 0)
        def _():
            for i in (2, 4, 6):
                wait_gain(i).wait_recv()
            for copy in weight_copies[7:9]:
                copy.wait()
            for i in range(2):
                wait_other(i)

        def chip_at(j):
            return lax.rem(x_chip + j + (j // 2) * (5 - 2 * j), 4)

        def collect(xc, own):
            for i in (1, 3, 2) if own else (1, 3, 2, 0):
                q = col_at(i)
                remote(
                    x2_all.at[xc, q], x2_all.at[xc, q], send5.at[1], recv5.at[xc, q],
                    (s, pair, c),
                ).wait_recv()
            values = x2_all[xc].reshape(STREAMS, WIDE).astype(f32)
            square = values * values
            squares = square[:, 0:128]
            for k in range(1, 5):
                squares = squares + square[:, k * 128:(k + 1) * 128]
            return (values * gain2[2 * xc + core, 0:1]).astype(bf16), squares

        def gate_part(scaled, xc, h):
            return jnp.dot(scaled, wgu[h, xc], preferred_element_type=f32)

        scaled, squares = collect(x_chip, True)
        for h in range(2):
            acc[h] = gate_part(scaled, x_chip, h)

        def gate_step(j, squares):
            xc = chip_at(j)
            scaled, more = collect(xc, False)
            for h in range(2):
                acc[h] += gate_part(scaled, xc, h)
            return squares + more

        squares = lax.fori_loop(1, CHIPS - 1, gate_step, squares)

        def swap(h):
            return remote(
                mine.at[h], theirs.at[h], send_p.at[h], recv_p.at[h], (s, pair, c)
            )

        far = chip_at(CHIPS - 1)
        scaled, more = collect(far, False)
        squares = jnp.sum(squares + more, axis=1, keepdims=True)
        high = squares.astype(bf16).astype(f32)
        sums = jnp.where(lane < 64, high, squares - high)
        for h in range(2):
            product = acc[h] + gate_part(scaled, far, h)
            acc[h] = product
            mine[h] = jnp.concatenate([product, sums], axis=1).astype(bf16)
            swap(h).start()
        @pl.when(t == 0)
        def _():
            for copy in weight_copies[9:13]:
                copy.wait()
            for i in range(2, 6):
                wait_other(i)

        def down_columns(xc):
            return pl.ds(pl.multiple_of(xc * WIDE, WIDE), WIDE)

        activations = []
        for h in range(2):
            swap(h).wait_recv()
            other = theirs[h].astype(f32)
            if h == 0:
                tail = other[:, 1024:1152]
                mean_square = (squares + tail[:, 0:1] + tail[:, 64:65]) / D
                scale = lax.rsqrt(mean_square + norm_eps)
            both = (acc[h] + other[:, 0:1024]) * scale
            gate, up = both[:, 0:HIDDEN], both[:, HIDDEN:2 * HIDDEN]
            half = 0.5 * gate
            activations.append(((half + half * jnp.tanh(half)) * up).astype(bf16))
            if h == 0:
                far_part = jnp.dot(
                    activations[0], wd[0, :, down_columns(far)], preferred_element_type=f32
                )
        activation = jnp.concatenate(activations, axis=1)

        def send_six(xc, i):
            q = col_at(i)
            return remote(
                s6.at[xc, q], r6.at[x_chip, c], send6.at[xc, i], recv6.at[x_chip, c],
                (s, 2 * xc + core, q),
            )

        def send_part(xc, part):
            s6[xc] = part.astype(bf16).reshape(COLS, SUB, WIDE)
            for i in (2, 1, 3):
                send_six(xc, i).start()

            @pl.when(xc != x_chip)
            def _():
                send_six(xc, 0).start()

        def down_step(j, _):
            xc = lax.rem(x_chip + lax.rem(2 * j + 2, 4) + j // 2, CHIPS)
            columns = wd[:, :, down_columns(xc)].reshape(2 * HIDDEN, WIDE)
            send_part(xc, jnp.dot(activation, columns, preferred_element_type=f32))
            return 0

        far_part = far_part + jnp.dot(
            activations[1], wd[1, :, down_columns(far)], preferred_element_type=f32
        )
        send_part(far, far_part)
        lax.fori_loop(1, CHIPS, down_step, 0)

        def sum_step(j, total):
            xc = chip_at(j)
            for i in (1, 3, 2):
                q = col_at(i)
                remote(
                    s6.at[xc, q], r6.at[xc, q], send6.at[xc, i], recv6.at[xc, q],
                    (s, pair, c),
                ).wait_recv()
                total = total + r6[xc, q].astype(f32)
            return total

        total = sum_step(0, after + s6[x_chip, c].astype(f32))

        def far_step(j, total):
            xc = chip_at(j)
            remote(
                s6.at[xc, c], r6.at[xc, c], send6.at[xc, 0], recv6.at[xc, c], (s, pair, c)
            ).wait_recv()
            return sum_step(j, total + r6[xc, c].astype(f32))

        total = lax.fori_loop(1, CHIPS, far_step, total)
        x_send[...] = total.astype(bf16)

        def send_one(i):
            return remote(
                x_send, xin.at[t + 1, c], send1.at[i], recv1.at[t, c],
                (s_next, r, col_at(i)),
            )

        def wait_one(i):
            return remote(
                x_send, xin.at[t + 1, col_at(i)], send1.at[i], recv1.at[t, col_at(i)],
                (s_next, r, col_at(i)),
            )

        @pl.when(t == 0)
        def _():
            pl.semaphore_wait(zready, 1)

        for i in (2, 1, 3, 0):
            send_one(i).start()

        for g in range(KVSPLIT):
            for i in range(1, ROWS):
                send_two(g, i).wait_send()
                send_three(g, i).wait_send()
        for i in range(1, COLS):
            send_four(i).wait_send()

        for i in range(1, PEERS):
            send_five(i).wait_send()
        for h in range(2):
            swap(h).wait_send()
        for i in range(CHIPS):
            for k in range(1, COLS):
                send_six(i, k).wait_send()

            @pl.when(i != x_chip)
            def _():
                send_six(i, 0).wait_send()

        for i in range(COLS):
            send_one(i).wait_send()
        for i in range(COLS):
            wait_one(i).wait_recv()
        return 0

    lax.fori_loop(0, TURNS, turn, 0)

    final = xin[TURNS].reshape(STREAMS, WIDE).astype(f32)
    final = pltpu.roll(final, lax.rem(WIDE - c * PIECE, WIDE), 1)
    out_ref[0] = final[:, 0:PIECE].astype(bf16)
    for i in range(1, COLS):
        send_init(i).wait_send()
    for i in (2, 4, 6):
        send_gain(i).wait_send()
    for copy in other_copies:
        copy.wait_send()


def per_device(
    hidden,
    lengths,
    attn_gain,
    ffn_gain,
    q_weight,
    key_weight,
    value_weight,
    out_weight,
    gate_weight,
    up_weight,
    down_weight,
    key_cache,
    value_cache,
):
    vmem = pl.BlockSpec(memory_space=pltpu.VMEM)
    hbm = pl.BlockSpec(memory_space=pl.ANY)
    dma = pltpu.SemaphoreType.DMA
    return pl.pallas_call(
        kernel,
        out_shape=pltpu.VMEM((1, STREAMS, PIECE), bf16),
        in_specs=[hbm] * 13,
        out_specs=vmem,
        scratch_shapes=[
            pltpu.SMEM((TURNS, LOCAL), jnp.int32),
            pltpu.VMEM((1, STREAMS, PIECE), bf16),
            pltpu.VMEM((1, PIECE), bf16),
            pltpu.VMEM((1, PIECE), bf16),
            pltpu.VMEM((WIDE, KVSPLIT * QKV), bf16),
            pltpu.VMEM((1280, WIDE), bf16),
            pltpu.VMEM((2, CHIPS, WIDE, 2 * HIDDEN), bf16),
            pltpu.VMEM((2, HIDDEN, CHIPS * WIDE), bf16),
            pltpu.VMEM((TURNS, 2, LOCAL, CTX, HD), bf16),
            pltpu.VMEM((TURNS, 2, LOCAL, CTX, HD), bf16),
            pltpu.VMEM((COLS, 80, 256), bf16),
            pltpu.VMEM((1, WIDE), f32),
            pltpu.VMEM((ROWS, 8, WIDE), f32),
            pltpu.VMEM((TURNS, LOCAL, LOCAL * CTX), f32),
            pltpu.VMEM((TURNS + 1, COLS, SUB, WIDE), bf16),
            pltpu.VMEM((KVSPLIT, ROWS, SUB, PACK), bf16),
            pltpu.VMEM((KVSPLIT, ROWS, SUB, PACK), bf16),
            pltpu.VMEM((KVSPLIT, ROWS, SUB, OPACK), bf16),
            pltpu.VMEM((COLS, SUB, WIDE), bf16),
            pltpu.VMEM((COLS, SUB, WIDE), bf16),
            pltpu.VMEM((CHIPS, COLS, SUB, WIDE), bf16),
            pltpu.VMEM((2, STREAMS, 2 * HIDDEN), f32),
            pltpu.VMEM((2, STREAMS, 2 * HIDDEN + 128), bf16),
            pltpu.VMEM((2, STREAMS, 2 * HIDDEN + 128), bf16),
            pltpu.VMEM((CHIPS, COLS, SUB, WIDE), bf16),
            pltpu.VMEM((CHIPS, COLS, SUB, WIDE), bf16),
            pltpu.VMEM((SUB, WIDE), bf16),
            dma((4,)),
            dma((13,)),
            dma((TURNS, 4)),
            pltpu.SemaphoreType.REGULAR,
            dma((COLS,)),
            dma((COLS,)),
            dma((ROWS,)),
            dma((ROWS,)),
            dma((COLS,)),
            dma((TURNS, COLS)),
            dma((KVSPLIT, ROWS)),
            dma((KVSPLIT, ROWS)),
            dma((KVSPLIT, ROWS)),
            dma((KVSPLIT, ROWS)),
            dma((COLS,)),
            dma((COLS,)),
            dma((PEERS,)),
            dma((CHIPS, COLS)),
            dma((2,)),
            dma((2,)),
            dma((6,)),
            dma((6,)),
            dma((CHIPS, COLS)),
            dma((CHIPS, COLS)),
        ],
        compiler_params=pltpu.CompilerParams(
            collective_id=0, has_side_effects=True, vmem_limit_bytes=56 * 1024 * 1024
        ),
        cost_estimate=pl.CostEstimate(
            flops=TURNS * 2 * STREAMS * 9830400, bytes_accessed=24_000_000, transcendentals=0
        ),
    )(
        lengths,
        hidden,
        attn_gain,
        ffn_gain,
        q_weight,
        key_weight,
        value_weight,
        out_weight,
        gate_weight.reshape(CHIPS, 2, WIDE, HIDDEN),
        up_weight.reshape(CHIPS, 2, WIDE, HIDDEN),
        down_weight,
        key_cache,
        value_cache,
    )


def solution(mesh):
    return jax.shard_map(
        per_device,
        mesh=mesh,
        in_specs=(
            P("section", None, ("row", "col")),
            P(None, "row"),
            P("section", ("row", "col")),
            P("section", ("row", "col")),
            P("section", "row", "col"),
            P("section", "row", "col"),
            P("section", "row", "col"),
            P("section", "col", "row"),
            P("section", None, ("row", "col")),
            P("section", None, ("row", "col")),
            P("section", ("row", "col"), None),
            P("section", None, "row", "col", None, None),
            P("section", None, "row", "col", None, None),
        ),
        out_specs=P("section", None, ("row", "col")),
        check_vma=False,
    )
```

```python
import functools
import math

import jax
import jax.numpy as jnp
from jax import lax
from jax.experimental import pallas as pl
from jax.experimental.pallas import tpu as pltpu
from jax.sharding import PartitionSpec as P

D = 5120
HD = 128
CTX = 96
TURNS = 4
ROWS = 8
COLS = 4
CHIPS = 4
PEERS = 16
WIDE = 640
PIECE = 160
SUB = 16
STREAMS = 64
LOCAL = 8
KVSPLIT = 2
QKV = 896
PACK = 512
OPACK = 384
HIDDEN = 512
norm_eps = 1e-06
masked_score = -1e30
f32 = jnp.float32
bf16 = jnp.bfloat16


def remote(src, dst, send, recv, device):
    return pltpu.make_async_remote_copy(
        src_ref=src,
        dst_ref=dst,
        send_sem=send,
        recv_sem=recv,
        device_id=device,
        device_id_type=pl.DeviceIdType.MESH,
    )


def kernel(
    len_hbm,
    hid_hbm,
    ag_hbm,
    fg_hbm,
    wq_hbm,
    wk_hbm,
    wv_hbm,
    wo_hbm,
    wg_hbm,
    wu_hbm,
    wd_hbm,
    kc_hbm,
    vc_hbm,
    out_ref,
    len_ref,
    hid_ref,
    ag_ref,
    fg_ref,
    wqkv,
    wo,
    wgu,
    wd,
    kc,
    vc,
    stage,
    init,
    gain1,
    gain2,
    bias,
    xin,
    s2,
    r2,
    o3,
    s4,
    r4,
    x2_all,
    acc,
    mine,
    theirs,
    s6,
    r6,
    x_send,
    isem,
    wsem,
    csem,
    zready,
    send0,
    recv0,
    sendg,
    recvg,
    send1,
    recv1,
    send2,
    recv2,
    send3,
    recv3,
    send4,
    recv4,
    send5,
    recv5,
    send_p,
    recv_p,
    send_w,
    recv_w,
    send6,
    recv6,
):
    s = lax.axis_index("section")
    r = lax.axis_index("row")
    c = lax.axis_index("col")
    x_chip = r // 2
    core = lax.rem(r, 2)
    pair = 2 * x_chip + 1 - core
    s_next = lax.rem(s + 1, TURNS)
    s_prev = lax.rem(s + TURNS - 1, TURNS)

    def row_at(i):
        return lax.rem(r + i, ROWS)

    def col_at(i):
        return lax.rem(c + i, COLS)

    inputs = [
        pltpu.make_async_copy(hid_hbm, hid_ref, isem.at[0]),
        pltpu.make_async_copy(ag_hbm, ag_ref, isem.at[1]),
        pltpu.make_async_copy(fg_hbm, fg_ref, isem.at[2]),
        pltpu.make_async_copy(len_hbm, len_ref, isem.at[3]),
    ]
    weight_copies = []
    for g in range(KVSPLIT):
        for source, first, width in ((wq_hbm, 0, WIDE), (wk_hbm, WIDE, HD), (wv_hbm, WIDE + HD, HD)):
            weight_copies.append(
                pltpu.make_async_copy(
                    source.at[0, :, pl.ds(g * width, width)],
                    wqkv.at[:, pl.ds(g * QKV + first, width)],
                    wsem.at[len(weight_copies)],
                )
            )
    weight_copies += [
        pltpu.make_async_copy(wo_hbm.at[0], wo, wsem.at[6]),
        pltpu.make_async_copy(
            wg_hbm.at[:, core], wgu.at[core, :, :, pl.ds(0, HIDDEN)], wsem.at[7]
        ),
        pltpu.make_async_copy(
            wu_hbm.at[:, core], wgu.at[core, :, :, pl.ds(HIDDEN, HIDDEN)], wsem.at[8]
        ),
    ]
    other_copies = [
        remote(
            wg_hbm.at[:, 1 - core], wgu.at[core, :, :, pl.ds(0, HIDDEN)],
            send_w.at[0], recv_w.at[0], (s, pair, c),
        ),
        remote(
            wu_hbm.at[:, 1 - core], wgu.at[core, :, :, pl.ds(HIDDEN, HIDDEN)],
            send_w.at[1], recv_w.at[1], (s, pair, c),
        ),
    ]
    for i in range(CHIPS):
        ours = pl.multiple_of((2 * i + core) * WIDE, WIDE)
        other = pl.multiple_of((2 * i + 1 - core) * WIDE, WIDE)
        weight_copies.append(
            pltpu.make_async_copy(
                wd_hbm.at[0, :, pl.ds(ours, WIDE)],
                wd.at[core, :, pl.ds(i * WIDE, WIDE)],
                wsem.at[9 + i],
            )
        )
        other_copies.append(
            remote(
                wd_hbm.at[0, :, pl.ds(other, WIDE)], wd.at[core, :, pl.ds(i * WIDE, WIDE)],
                send_w.at[2 + i], recv_w.at[2 + i], (s, pair, c),
            )
        )

    def wait_other(i):
        if i < 2:
            place = wgu.at[1 - core, :, :, pl.ds(i * HIDDEN, HIDDEN)]
        else:
            place = wd.at[1 - core, :, pl.ds((i - 2) * WIDE, WIDE)]
        remote(place, place, send_w.at[i], recv_w.at[i], (s, pair, c)).wait_recv()

    def cache_copies(t):
        m = lax.rem(s + TURNS - t, TURNS)
        copies = []
        for g in range(2):
            copies.append(
                pltpu.make_async_copy(kc_hbm.at[0, m, :, g], kc.at[t, g], csem.at[t, g])
            )
            copies.append(
                pltpu.make_async_copy(vc_hbm.at[0, m, :, g], vc.at[t, g], csem.at[t, 2 + g])
            )
        return copies

    barrier = pltpu.get_barrier_semaphore()
    greeted = [(s, row_at(i), c) for i in range(1, ROWS)]
    greeted += [(s, r, col_at(i)) for i in range(1, COLS)]
    greeted += [(s_prev, r, c), (s_next, r, c)]
    for device in greeted:
        pl.semaphore_signal(
            barrier, inc=1, device_id=device, device_id_type=pl.DeviceIdType.MESH
        )

    def row_of(dx):
        return 2 * lax.rem(x_chip + dx, CHIPS) + core

    for copy in inputs + weight_copies[:6]:
        copy.start()
    for copy in cache_copies(0):
        copy.start()
    for copy in weight_copies[6:]:
        copy.start()
    for t in range(1, TURNS):
        for copy in cache_copies(t):
            copy.start()
    for copy in inputs:
        copy.wait()

    stage[...] = jnp.zeros((80, 256), bf16)
    stage[0:64, 0:PIECE] = hid_ref[0]
    gain_row = lax.broadcasted_iota(jnp.int32, (SUB, PIECE), 0)
    stage[64:80, 0:PIECE] = jnp.where(
        gain_row == 0, ag_ref[...].astype(f32), fg_ref[...].astype(f32)
    ).astype(bf16)

    ends = stage[:, 128:256].astype(f32)
    packed = ends[0:16]
    for i in range(1, 4):
        packed = packed + pltpu.roll(ends[16 * i:16 * i + 16], 32 * i, 1)
    init[c, 0:80] = stage[:, 0:128]
    init[c, 80:112] = jnp.concatenate([packed, ends[64:80]], axis=0).astype(bf16)

    pl.semaphore_wait(barrier, len(greeted))

    def send_init(i):
        return remote(
            init.at[c], init.at[c], send0.at[i], recv0.at[c], (s, r, col_at(i))
        )

    def wait_init(i):
        return remote(
            init.at[col_at(i)], init.at[col_at(i)], send0.at[i], recv0.at[col_at(i)],
            (s, r, col_at(i)),
        )

    for i in (2, 1, 3):
        send_init(i).start()
    for copy in other_copies[:1]:
        copy.start()
    stream_row = lax.broadcasted_iota(jnp.int32, (LOCAL, LOCAL * CTX), 0)
    position = lax.broadcasted_iota(jnp.int32, (LOCAL, LOCAL * CTX), 1)
    for t in range(TURNS):
        m = lax.rem(s + TURNS - t, TURNS)
        offsets = jnp.full((LOCAL, LOCAL * CTX), masked_score, f32)
        for b in range(LOCAL):
            live = (
                (stream_row == b)
                & (position >= b * CTX)
                & (position < b * CTX + len_ref[m, b])
            )
            offsets = jnp.where(live, 0.0, offsets)
        bias[t] = offsets

    for i in range(1, COLS):
        wait_init(i).wait_recv()
    pl.semaphore_signal(
        zready, inc=1, device_id=(s_prev, r, c), device_id_type=pl.DeviceIdType.MESH
    )
    joined = None
    for i in range(COLS):
        message = init[i].astype(f32)
        packed = message[80:96]
        ends = jnp.concatenate(
            [packed] + [pltpu.roll(packed, 128 - 32 * k, 1) for k in range(1, 4)]
            + [message[96:112]],
            axis=0,
        )
        end_lane = lax.broadcasted_iota(jnp.int32, (80, 128), 1)
        ends = jnp.where(end_lane < PIECE - 128, ends, 0.0)
        piece = jnp.concatenate(
            [message[0:80], ends, jnp.zeros((80, WIDE - 256), f32)], axis=1
        )
        if i:
            piece = pltpu.roll(piece, i * PIECE, 1)
        joined = piece if joined is None else joined + piece
    xin[0] = joined[0:64].astype(bf16).reshape(COLS, SUB, WIDE)
    gain1[...] = joined[64:65]
    gain2[r] = jnp.broadcast_to(joined[65:66], (8, WIDE))

    def send_gain(i):
        return remote(
            gain2.at[r], gain2.at[r], sendg.at[i], recvg.at[r], (s, row_at(i), c)
        )

    def wait_gain(i):
        return remote(
            gain2.at[row_at(i)], gain2.at[row_at(i)], sendg.at[i], recvg.at[row_at(i)],
            (s, row_at(i), c),
        )

    def turn(t, _):
        x_all = xin[t].reshape(STREAMS, WIDE).astype(f32)
        squares = jnp.sum(x_all * x_all, axis=1, keepdims=True)
        high = squares.astype(bf16).astype(f32)
        low = squares - high
        left = (x_all * gain1[...]).astype(bf16)

        @pl.when(t == 0)
        def _():
            for copy in weight_copies[:6]:
                copy.wait()

        lane = lax.broadcasted_iota(jnp.int32, (STREAMS, 128), 1)
        sums = jnp.where(lane < 64, high, low).reshape(ROWS, LOCAL, 128)

        def send_two(g, i):
            return remote(
                s2.at[g, row_at(i)], r2.at[g, r], send2.at[g, i], recv2.at[g, r],
                (s, row_at(i), c),
            )

        def wait_two(g, i):
            return remote(
                s2.at[g, row_at(i)], r2.at[g, row_at(i)], send2.at[g, i],
                recv2.at[g, row_at(i)], (s, row_at(i), c),
            )

        for g in range(KVSPLIT):
            part = jnp.dot(
                left, wqkv[:, g * QKV:(g + 1) * QKV], preferred_element_type=f32
            ).reshape(ROWS, LOCAL, QKV)
            rest = jnp.concatenate([part[:, :, PACK:QKV], sums], axis=2)
            s2[g] = jnp.concatenate([part[:, :, 0:PACK], rest], axis=1).astype(bf16)
            for i in (4, 3, 5, 2, 6, 1, 7):
                send_two(g, i).start()

        @pl.when(t == 0)
        def _():
            for i in (2, 4, 6):
                send_gain(i).start()
            other_copies[1].start()

        @pl.when(t == 0)
        def _():
            for copy in cache_copies(0):
                copy.wait()

        @pl.when(t > 0)
        def _():
            for copy in cache_copies(t):
                copy.wait()

        def send_three(g, i):
            return remote(
                o3.at[g, r], o3.at[g, r], send3.at[g, i], recv3.at[g, r], (s, row_at(i), c)
            )

        def wait_three(g, i):
            return remote(
                o3.at[g, row_at(i)], o3.at[g, row_at(i)], send3.at[g, i],
                recv3.at[g, row_at(i)], (s, row_at(i), c),
            )

        score_scale = 1.0 / math.sqrt(HD)
        offsets = jnp.concatenate([bias[t]] * 5, axis=0)
        for g in range(KVSPLIT):
            total = s2[g, r].astype(f32)
            for i in (1, 7, 2, 6, 3, 5, 4):
                wait_two(g, i).wait_recv()
                total = total + r2[g, row_at(i)].astype(f32)
            top, bottom = total[0:8], total[8:16]
            mean_square = (bottom[:, 384:385] + bottom[:, 448:449]) / D
            scale = lax.rsqrt(mean_square + norm_eps)
            top = (top * scale).astype(bf16).astype(f32)
            bottom = (bottom[:, 0:384] * scale).astype(bf16).astype(f32)
            queries = jnp.concatenate(
                [top[:, j * HD:(j + 1) * HD] for j in range(4)] + [bottom[:, 0:HD]], axis=0
            )
            key_new = jnp.concatenate([bottom[:, HD:2 * HD]] * 5, axis=0)
            value_new = jnp.concatenate([bottom[:, 2 * HD:3 * HD]] * 5, axis=0)
            keys = kc[t, g].reshape(LOCAL * CTX, HD)
            values = vc[t, g].reshape(LOCAL * CTX, HD)
            scores = lax.dot_general(
                queries.astype(bf16), keys, (((1,), (1,)), ((), ())),
                preferred_element_type=f32,
            )
            scores = scores * score_scale + offsets
            self_score = jnp.sum(queries * key_new, axis=1, keepdims=True) * score_scale
            row_max = jnp.maximum(jnp.max(scores, axis=1, keepdims=True), self_score)
            weights = jnp.exp(scores - row_max)
            self_weight = jnp.exp(self_score - row_max)
            denominator = jnp.sum(weights, axis=1, keepdims=True) + self_weight
            share = 1.0 / denominator
            probs = (weights * share).astype(bf16)
            self_prob = (self_weight * share).astype(bf16).astype(f32)
            mixed = jnp.dot(probs, values, preferred_element_type=f32)
            mixed = mixed + self_prob * value_new
            heads = [mixed[j * 8:(j + 1) * 8] for j in range(5)]
            o3[g, r] = jnp.concatenate(
                [
                    jnp.concatenate(heads[0:3], axis=1),
                    jnp.concatenate(heads[3:5] + [jnp.zeros((LOCAL, HD), f32)], axis=1),
                ],
                axis=0,
            ).astype(bf16)
            for i in (4, 3, 5, 2, 6, 1, 7):
                send_three(g, i).start()

        @pl.when(t == 0)
        def _():
            weight_copies[6].wait()
            for copy in other_copies[2:]:
                copy.start()

        out_part = None
        for g in range(KVSPLIT):
            for i in (1, 7, 2, 6, 3, 5, 4):
                wait_three(g, i).wait_recv()
            gathered = o3[g].astype(f32)
            heads = jnp.concatenate(
                [
                    gathered[:, 0:8].reshape(STREAMS, OPACK),
                    gathered[:, 8:16, 0:WIDE - OPACK].reshape(STREAMS, WIDE - OPACK),
                ],
                axis=1,
            ).astype(bf16)
            product = jnp.dot(
                heads, wo[g * WIDE:(g + 1) * WIDE, :], preferred_element_type=f32
            )
            out_part = product if out_part is None else out_part + product
        s4[...] = out_part.astype(bf16).reshape(COLS, SUB, WIDE)

        def send_four(i):
            return remote(
                s4.at[col_at(i)], r4.at[c], send4.at[i], recv4.at[c], (s, r, col_at(i))
            )

        def wait_four(i):
            return remote(
                s4.at[col_at(i)], r4.at[col_at(i)], send4.at[i], recv4.at[col_at(i)],
                (s, r, col_at(i)),
            )

        for i in (2, 1, 3):
            send_four(i).start()
        after = xin[t, c].astype(f32) + s4[c].astype(f32)
        for i in (1, 3, 2):
            wait_four(i).wait_recv()
            after = after + r4[col_at(i)].astype(f32)
        x2_all[x_chip, c] = after.astype(bf16)
        after = x2_all[x_chip, c].astype(f32)

        def send_five(i):
            return remote(
                x2_all.at[x_chip, c], x2_all.at[x_chip, c], send5.at[i], recv5.at[x_chip, c],
                (s, row_of(i // COLS), col_at(i % COLS)),
            )

        for i in (2, 1, 3, 6, 14, 5, 7, 13, 15, 4, 12, 10, 9, 11, 8):
            send_five(i).start()

        @pl.when(t == 0)
        def _():
            for i in (2, 4, 6):
                wait_gain(i).wait_recv()
            for copy in weight_copies[7:9]:
                copy.wait()
            for i in range(2):
                wait_other(i)

        def chip_at(j):
            return lax.rem(x_chip + j + (j // 2) * (5 - 2 * j), 4)

        def collect(xc, own):
            for i in (1, 3, 2) if own else (1, 3, 2, 0):
                q = col_at(i)
                remote(
                    x2_all.at[xc, q], x2_all.at[xc, q], send5.at[1], recv5.at[xc, q],
                    (s, pair, c),
                ).wait_recv()
            values = x2_all[xc].reshape(STREAMS, WIDE).astype(f32)
            square = values * values
            squares = square[:, 0:128]
            for k in range(1, 5):
                squares = squares + square[:, k * 128:(k + 1) * 128]
            return (values * gain2[2 * xc + core, 0:1]).astype(bf16), squares

        def gate_part(scaled, xc, h):
            return jnp.dot(scaled, wgu[h, xc], preferred_element_type=f32)

        scaled, squares = collect(x_chip, True)
        for h in range(2):
            acc[h] = gate_part(scaled, x_chip, h)

        def gate_step(j, squares):
            xc = chip_at(j)
            scaled, more = collect(xc, False)
            for h in range(2):
                acc[h] += gate_part(scaled, xc, h)
            return squares + more

        squares = lax.fori_loop(1, CHIPS - 1, gate_step, squares)

        def swap(h):
            return remote(
                mine.at[h], theirs.at[h], send_p.at[h], recv_p.at[h], (s, pair, c)
            )

        far = chip_at(CHIPS - 1)
        scaled, more = collect(far, False)
        squares = jnp.sum(squares + more, axis=1, keepdims=True)
        high = squares.astype(bf16).astype(f32)
        sums = jnp.where(lane < 64, high, squares - high)
        for h in range(2):
            product = acc[h] + gate_part(scaled, far, h)
            acc[h] = product
            mine[h] = jnp.concatenate([product, sums], axis=1).astype(bf16)
            swap(h).start()
        @pl.when(t == 0)
        def _():
            for copy in weight_copies[9:13]:
                copy.wait()
            for i in range(2, 6):
                wait_other(i)

        def down_columns(xc):
            return pl.ds(pl.multiple_of(xc * WIDE, WIDE), WIDE)

        activations = []
        for h in range(2):
            swap(h).wait_recv()
            other = theirs[h].astype(f32)
            if h == 0:
                tail = other[:, 1024:1152]
                mean_square = (squares + tail[:, 0:1] + tail[:, 64:65]) / D
                scale = lax.rsqrt(mean_square + norm_eps)
            both = (acc[h] + other[:, 0:1024]) * scale
            gate, up = both[:, 0:HIDDEN], both[:, HIDDEN:2 * HIDDEN]
            half = 0.5 * gate
            activations.append(((half + half * jnp.tanh(half)) * up).astype(bf16))
            if h == 0:
                far_part = jnp.dot(
                    activations[0], wd[0, :, down_columns(far)], preferred_element_type=f32
                )
        activation = jnp.concatenate(activations, axis=1)

        def send_six(xc, i):
            q = col_at(i)
            return remote(
                s6.at[xc, q], r6.at[x_chip, c], send6.at[xc, i], recv6.at[x_chip, c],
                (s, 2 * xc + core, q),
            )

        def send_part(xc, part):
            s6[xc] = part.astype(bf16).reshape(COLS, SUB, WIDE)
            for i in (2, 1, 3):
                send_six(xc, i).start()

            @pl.when(xc != x_chip)
            def _():
                send_six(xc, 0).start()

        def down_step(j, _):
            xc = lax.rem(x_chip + lax.rem(2 * j + 2, 4) + j // 2, CHIPS)
            columns = wd[:, :, down_columns(xc)].reshape(2 * HIDDEN, WIDE)
            send_part(xc, jnp.dot(activation, columns, preferred_element_type=f32))
            return 0

        far_part = far_part + jnp.dot(
            activations[1], wd[1, :, down_columns(far)], preferred_element_type=f32
        )
        send_part(far, far_part)
        lax.fori_loop(1, CHIPS, down_step, 0)

        def sum_step(j, total):
            xc = chip_at(j)
            for i in (1, 3, 2):
                q = col_at(i)
                remote(
                    s6.at[xc, q], r6.at[xc, q], send6.at[xc, i], recv6.at[xc, q],
                    (s, pair, c),
                ).wait_recv()
                total = total + r6[xc, q].astype(f32)
            return total

        total = sum_step(0, after + s6[x_chip, c].astype(f32))

        def far_step(j, total):
            xc = chip_at(j)
            remote(
                s6.at[xc, c], r6.at[xc, c], send6.at[xc, 0], recv6.at[xc, c], (s, pair, c)
            ).wait_recv()
            return sum_step(j, total + r6[xc, c].astype(f32))

        total = lax.fori_loop(1, CHIPS, far_step, total)
        x_send[...] = total.astype(bf16)

        def send_one(i):
            return remote(
                x_send, xin.at[t + 1, c], send1.at[i], recv1.at[t, c],
                (s_next, r, col_at(i)),
            )

        def wait_one(i):
            return remote(
                x_send, xin.at[t + 1, col_at(i)], send1.at[i], recv1.at[t, col_at(i)],
                (s_next, r, col_at(i)),
            )

        @pl.when(t == 0)
        def _():
            pl.semaphore_wait(zready, 1)

        for i in (2, 1, 3, 0):
            send_one(i).start()

        for g in range(KVSPLIT):
            for i in range(1, ROWS):
                send_two(g, i).wait_send()
                send_three(g, i).wait_send()
        for i in range(1, COLS):
            send_four(i).wait_send()

        for i in range(1, PEERS):
            send_five(i).wait_send()
        for h in range(2):
            swap(h).wait_send()
        for i in range(CHIPS):
            for k in range(1, COLS):
                send_six(i, k).wait_send()

            @pl.when(i != x_chip)
            def _():
                send_six(i, 0).wait_send()

        for i in range(COLS):
            send_one(i).wait_send()
        for i in range(COLS):
            wait_one(i).wait_recv()
        return 0

    lax.fori_loop(0, TURNS, turn, 0)

    final = xin[TURNS].reshape(STREAMS, WIDE).astype(f32)
    final = pltpu.roll(final, lax.rem(WIDE - c * PIECE, WIDE), 1)
    out_ref[0] = final[:, 0:PIECE].astype(bf16)
    for i in range(1, COLS):
        send_init(i).wait_send()
    for i in (2, 4, 6):
        send_gain(i).wait_send()
    for copy in other_copies:
        copy.wait_send()


def per_device(
    hidden,
    lengths,
    attn_gain,
    ffn_gain,
    q_weight,
    key_weight,
    value_weight,
    out_weight,
    gate_weight,
    up_weight,
    down_weight,
    key_cache,
    value_cache,
):
    vmem = pl.BlockSpec(memory_space=pltpu.VMEM)
    hbm = pl.BlockSpec(memory_space=pl.ANY)
    dma = pltpu.SemaphoreType.DMA
    return pl.pallas_call(
        kernel,
        out_shape=pltpu.VMEM((1, STREAMS, PIECE), bf16),
        in_specs=[hbm] * 13,
        out_specs=vmem,
        scratch_shapes=[
            pltpu.SMEM((TURNS, LOCAL), jnp.int32),
            pltpu.VMEM((1, STREAMS, PIECE), bf16),
            pltpu.VMEM((1, PIECE), bf16),
            pltpu.VMEM((1, PIECE), bf16),
            pltpu.VMEM((WIDE, KVSPLIT * QKV), bf16),
            pltpu.VMEM((1280, WIDE), bf16),
            pltpu.VMEM((2, CHIPS, WIDE, 2 * HIDDEN), bf16),
            pltpu.VMEM((2, HIDDEN, CHIPS * WIDE), bf16),
            pltpu.VMEM((TURNS, 2, LOCAL, CTX, HD), bf16),
            pltpu.VMEM((TURNS, 2, LOCAL, CTX, HD), bf16),
            pltpu.VMEM((80, 256), bf16),
            pltpu.VMEM((COLS, 112, 128), bf16),
            pltpu.VMEM((1, WIDE), f32),
            pltpu.VMEM((ROWS, 8, WIDE), f32),
            pltpu.VMEM((TURNS, LOCAL, LOCAL * CTX), f32),
            pltpu.VMEM((TURNS + 1, COLS, SUB, WIDE), bf16),
            pltpu.VMEM((KVSPLIT, ROWS, SUB, PACK), bf16),
            pltpu.VMEM((KVSPLIT, ROWS, SUB, PACK), bf16),
            pltpu.VMEM((KVSPLIT, ROWS, SUB, OPACK), bf16),
            pltpu.VMEM((COLS, SUB, WIDE), bf16),
            pltpu.VMEM((COLS, SUB, WIDE), bf16),
            pltpu.VMEM((CHIPS, COLS, SUB, WIDE), bf16),
            pltpu.VMEM((2, STREAMS, 2 * HIDDEN), f32),
            pltpu.VMEM((2, STREAMS, 2 * HIDDEN + 128), bf16),
            pltpu.VMEM((2, STREAMS, 2 * HIDDEN + 128), bf16),
            pltpu.VMEM((CHIPS, COLS, SUB, WIDE), bf16),
            pltpu.VMEM((CHIPS, COLS, SUB, WIDE), bf16),
            pltpu.VMEM((SUB, WIDE), bf16),
            dma((4,)),
            dma((13,)),
            dma((TURNS, 4)),
            pltpu.SemaphoreType.REGULAR,
            dma((COLS,)),
            dma((COLS,)),
            dma((ROWS,)),
            dma((ROWS,)),
            dma((COLS,)),
            dma((TURNS, COLS)),
            dma((KVSPLIT, ROWS)),
            dma((KVSPLIT, ROWS)),
            dma((KVSPLIT, ROWS)),
            dma((KVSPLIT, ROWS)),
            dma((COLS,)),
            dma((COLS,)),
            dma((PEERS,)),
            dma((CHIPS, COLS)),
            dma((2,)),
            dma((2,)),
            dma((6,)),
            dma((6,)),
            dma((CHIPS, COLS)),
            dma((CHIPS, COLS)),
        ],
        compiler_params=pltpu.CompilerParams(
            collective_id=0, has_side_effects=True, vmem_limit_bytes=56 * 1024 * 1024
        ),
        cost_estimate=pl.CostEstimate(
            flops=TURNS * 2 * STREAMS * 9830400, bytes_accessed=24_000_000, transcendentals=0
        ),
    )(
        lengths,
        hidden,
        attn_gain,
        ffn_gain,
        q_weight,
        key_weight,
        value_weight,
        out_weight,
        gate_weight.reshape(CHIPS, 2, WIDE, HIDDEN),
        up_weight.reshape(CHIPS, 2, WIDE, HIDDEN),
        down_weight,
        key_cache,
        value_cache,
    )


def solution(mesh):
    return jax.shard_map(
        per_device,
        mesh=mesh,
        in_specs=(
            P("section", None, ("row", "col")),
            P(None, "row"),
            P("section", ("row", "col")),
            P("section", ("row", "col")),
            P("section", "row", "col"),
            P("section", "row", "col"),
            P("section", "row", "col"),
            P("section", "col", "row"),
            P("section", None, ("row", "col")),
            P("section", None, ("row", "col")),
            P("section", ("row", "col"), None),
            P("section", None, "row", "col", None, None),
            P("section", None, "row", "col", None, None),
        ),
        out_specs=P("section", None, ("row", "col")),
        check_vma=False,
    )
```
